32 devices in a mesh: wide: 8 (over y, x, core), narrow: 4 (over z).
Axes of the slice: x: 2, y: 2, z: 4, core: 2. Of those that a mesh axis runs over, the one named last changes fastest.
Arguments:
- layer_input: bfloat16 [4, 1024, 2048], P('narrow', 'wide'), may hold values from -6 to 6
- output_grad: bfloat16 [4, 1024, 2048], P('narrow', 'wide'), may hold values from -6 to 6
- doc_ids: int32 [4, 1024], P('narrow'), may hold values from 0 to 2, as said below
- keep_mask: int32 [4, 1024], P('narrow'), may hold values from 0 to 1, as said below
- attention_gain: bfloat16 [2048], P(('wide', 'narrow')), may hold values from 0.099609375 to 1.8984375
- query_weight: bfloat16 [2048, 2048], P(('wide', 'narrow')), may hold values from -0.125 to 0.125
- key_weight: bfloat16 [2048, 512], P(('wide', 'narrow')), may hold values from -0.125 to 0.125
- value_weight: bfloat16 [2048, 512], P(('wide', 'narrow')), may hold values from -0.125 to 0.125
- out_weight: bfloat16 [2048, 2048], P(('wide', 'narrow')), may hold values from -2 to 2
- feedforward_gain: bfloat16 [2048], P(('wide', 'narrow')), may hold values from 0.099609375 to 1.8984375
- gate_weight: bfloat16 [2048, 8192], P(('wide', 'narrow')), may hold values from -0.125 to 0.125
- up_weight: bfloat16 [2048, 8192], P(('wide', 'narrow')), may hold values from -0.125 to 0.125
- down_weight: bfloat16 [8192, 2048], P(('wide', 'narrow')), may hold values from -0.0625 to 0.0625
Outputs:
- layer_output: bfloat16 [4, 1024, 2048], P('narrow', 'wide')
- input_grad: bfloat16 [4, 1024, 2048], P('narrow', 'wide')
- attention_gain_grad: float32 [2048], P(('wide', 'narrow'))
- query_grad: float32 [2048, 2048], P(('wide', 'narrow'))
- key_grad: float32 [2048, 512], P(('wide', 'narrow'))
- value_grad: float32 [2048, 512], P(('wide', 'narrow'))
- out_grad: float32 [2048, 2048], P(('wide', 'narrow'))
- feedforward_gain_grad: float32 [2048], P(('wide', 'narrow'))
- gate_grad: float32 [2048, 8192], P(('wide', 'narrow'))
- up_grad: float32 [2048, 8192], P(('wide', 'narrow'))
- down_grad: float32 [8192, 2048], P(('wide', 'narrow'))
The draws below stay inside these ranges and needn't reach their ends.
Inputs may be any that keep to these rules, and one draw needn't show every extreme that they name: `doc_ids`: in every stream document numbers never fall; document 0 ends within the first 128 tokens, document 2 begins within the last 128 tokens, and every document has a token. `keep_mask`: in every stream the zeros are one run at its end, inside document 2, after at least one token of it that is 1.
All inputs are finite; a program needn't handle non-finite values.
Results may differ from the reference program's by a relative error of at most 0.015.
Values may be sent and summed in bfloat16 or wider, within the bound.
No kernel may reach another device: no remote copies, remote signals or barrier semaphores. Data moves between devices by JAX's collectives and lax.ppermute only.
A program may use at most 640 MiB of HBM per device.

```python
import jax
import jax.numpy as jnp
import numpy as np
from jax import lax

D = 2048
HEADS = 32
HEAD = 64
FF = 8192
TOK_DEV = 128
DOCS = 3
KVD = 512
STREAMS = 4
STREAM_TOK = 1024


def stream_cuts(key):
    first_cut = jax.random.randint(jax.random.fold_in(key, 21), (STREAMS, 1), 1, TOK_DEV)
    second_cut = jax.random.randint(jax.random.fold_in(key, 22), (STREAMS, 1), STREAM_TOK - TOK_DEV + 1, STREAM_TOK - 2)
    pad_start = jax.random.randint(jax.random.fold_in(key, 23), (STREAMS, 1), second_cut + 1, STREAM_TOK)
    return (first_cut, second_cut, pad_start)


def draw_doc_ids(key, part):
    first_cut, second_cut, pad_start = stream_cuts(key)
    places = jnp.arange(STREAM_TOK, dtype=jnp.int32)[None, :]
    return (places >= first_cut).astype(jnp.int32) + (places >= second_cut).astype(jnp.int32)


def draw_keep_mask(key, part):
    first_cut, second_cut, pad_start = stream_cuts(key)
    places = jnp.arange(STREAM_TOK, dtype=jnp.int32)[None, :]
    return (places < pad_start).astype(jnp.int32)


def level_of(own_key, shape, shards, least, high):
    gain, own = 1.0, jax.random.fold_in(own_key, 6)
    for dim, shards_of in shards:
        heights = jnp.exp(jax.random.uniform(jax.random.fold_in(own, dim), (shards_of,), jnp.float32, least / len(shards), high / len(shards)))
        gain = gain * jnp.repeat(heights, shape[dim] // shards_of).reshape([-1 if axis == dim else 1 for axis in range(len(shape))])
    return gain


def scatter_about(key, shape, scale, limit, cuts=(), kind=jnp.bfloat16):
    gain = level_of(key, shape, cuts, -0.22, 0.18) if cuts else 1.0
    entries = jax.random.normal(key, shape, jnp.float32) * scale * gain
    return jnp.minimum(jnp.maximum(entries, -limit), limit).astype(kind)


def setup_inputs(seed: int = 0) -> dict:
    key_list = jax.random.split(jax.random.key(seed), 14)
    layer_input = scatter_about(key_list[0], (STREAMS, STREAM_TOK, D), 1.0, 6.0, ((0, 4), (1, 8)))
    output_grad = scatter_about(key_list[1], (STREAMS, STREAM_TOK, D), 1.0, 6.0, ((0, 4), (1, 8)))
    doc_ids = draw_doc_ids(jax.random.fold_in(key_list[13], 71), 0)
    keep_mask = draw_keep_mask(jax.random.fold_in(key_list[13], 71), 0)
    attention_gain = jnp.clip(1.0 + 0.18 * jax.random.normal(key_list[4], (D,), jnp.float32), 0.099609375, 1.8984375).astype(jnp.bfloat16)
    query_weight = scatter_about(key_list[5], (D, D), D ** -0.5, 0.125, ((0, 32),))
    key_weight = scatter_about(key_list[6], (D, KVD), D ** -0.5, 0.125, ((0, 32),))
    value_weight = scatter_about(key_list[7], (D, KVD), D ** -0.5, 0.125, ((0, 32),))
    out_weight = scatter_about(key_list[8], (D, D), (max(1, D * 4 // STREAM_TOK)) ** -0.5, 2.0, ((0, 32),))
    feedforward_gain = jnp.clip(1.0 + 0.18 * jax.random.normal(key_list[9], (D,), jnp.float32), 0.099609375, 1.8984375).astype(jnp.bfloat16)
    gate_weight = scatter_about(key_list[10], (D, FF), D ** -0.5, 0.125, ((0, 32),))
    up_weight = scatter_about(key_list[11], (D, FF), D ** -0.5, 0.125, ((0, 32),))
    down_weight = scatter_about(key_list[12], (FF, D), FF ** -0.5, 0.0625, ((0, 32),))
    return dict(layer_input=layer_input, output_grad=output_grad, doc_ids=doc_ids, keep_mask=keep_mask, attention_gain=attention_gain, query_weight=query_weight, key_weight=key_weight, value_weight=value_weight, out_weight=out_weight, feedforward_gain=feedforward_gain, gate_weight=gate_weight, up_weight=up_weight, down_weight=down_weight)


EPSILON = 1e-05
MASKED = -1e+30
HIGHEST = lax.Precision.HIGHEST

@jax.custom_vjp
def low(v):
    return lax.optimization_barrier(v.astype(jnp.bfloat16)).astype(jnp.float32)

@jax.custom_vjp
def low_back(v):
    return v

def low_keep(v):
    return (low(v), None)

def low_pass(kept, grad):
    return (grad,)

def back_keep(v):
    return (v, None)

def back_low(kept, grad):
    return (low(grad),)
low.defvjp(low_keep, low_pass)
low_back.defvjp(back_keep, back_low)

def inverse_rates(head_width):
    plain = 500000.0 ** (-(np.arange(0, head_width, 2) * 1.0) / head_width)
    wavelength = 2.0 * np.pi / plain
    smooth = (8192.0 / wavelength - 1.0) / 3.0
    blended = (1.0 - smooth) * plain / 32.0 + smooth * plain
    scaled = np.where(wavelength > 8192.0, plain / 32.0, np.where(wavelength < 2048.0, plain, blended))
    return scaled.astype(np.float32)

def turn_tables(positions):
    rates = jnp.asarray(inverse_rates(HEAD))
    angles = positions.astype(jnp.float32)[..., None] * rates
    angles = jnp.concatenate([angles, angles], axis=-1)
    return (jnp.cos(angles), jnp.sin(angles))

def rotate(values, cosine, sine_table):
    half_width = values.shape[-1] // 2
    turned = jnp.concatenate([-values[..., half_width:], values[..., :half_width]], axis=-1)
    return values * cosine[..., None, :] + turned * sine_table[..., None, :]

def stream_positions(documents):
    numbers = jnp.arange(DOCS, dtype=jnp.int32)
    starts = lax.optimization_barrier(jnp.sum((documents[None, :] < numbers[:, None]).astype(jnp.int32), axis=1))
    own_start = lax.optimization_barrier(jnp.sum(jnp.where(documents[:, None] == numbers[None, :], starts[None, :], 0), axis=1))
    return jnp.arange(documents.shape[0], dtype=jnp.int32) - own_start

def normalize(values):
    factor = lax.rsqrt(lax.optimization_barrier(jnp.mean(values * values, axis=-1, keepdims=True)) + EPSILON)
    return (values * factor, factor)

def attend_stream(queries, keys, values, documents, keep_flags):
    length = queries.shape[0]
    block_size = min(512, length)
    key_heads = keys.shape[1]
    group_size = queries.shape[1] // key_heads
    head_width = queries.shape[2]
    score_scale = head_width ** (-0.5)
    places = jnp.arange(length, dtype=jnp.int32)

    def one_block(pieces):
        query_block, query_places, query_docs = pieces
        grouped = query_block.reshape(block_size, key_heads, group_size, head_width)
        scores = low_back(jnp.einsum('tkgd,skd->kgts', grouped, keys, precision=HIGHEST) * score_scale)
        allowed = (query_docs[:, None] == documents[None, :]) & (places[None, :] <= query_places[:, None]) & (keep_flags[None, :] > 0)
        scores = jnp.where(allowed, scores, MASKED)
        shifted = jnp.exp(scores - lax.optimization_barrier(jnp.max(scores, axis=-1, keepdims=True)))
        weights = low(shifted / lax.optimization_barrier(jnp.sum(shifted, axis=-1, keepdims=True)))
        mixed = jnp.einsum('kgts,skd->tkgd', weights, values, precision=HIGHEST)
        return mixed.reshape(block_size, key_heads * group_size * head_width)
    pieces = (queries.reshape(length // block_size, block_size, queries.shape[1], head_width), places.reshape(-1, block_size), documents.reshape(-1, block_size))
    return lax.map(jax.checkpoint(one_block), pieces).reshape(length, -1)

def forward(inputs, attention_gain, query_weight, key_weight, value_weight, out_weight, feedforward_gain, gate_weight, up_weight, down_weight, documents, keep_flags):
    streams, length, model_width = inputs.shape
    key_heads = key_weight.shape[1] // HEAD
    cosine, sine_table = turn_tables(jax.vmap(stream_positions)(documents))
    flat_one = low(normalize(inputs)[0] * attention_gain).reshape(-1, model_width)
    query_lin = low_back(jnp.dot(flat_one, query_weight, precision=HIGHEST))
    key_lin = low_back(jnp.dot(flat_one, key_weight, precision=HIGHEST))
    value_lin = low_back(jnp.dot(flat_one, value_weight, precision=HIGHEST))
    queries = low(rotate(query_lin.reshape(streams, length, HEADS, HEAD), cosine, sine_table))
    keys = low(rotate(key_lin.reshape(streams, length, key_heads, HEAD), cosine, sine_table))
    values = low(value_lin.reshape(streams, length, key_heads, HEAD))
    attended = lax.map(jax.checkpoint(lambda pieces: attend_stream(*pieces)), (queries, keys, values, documents, keep_flags))
    mixed = low(low_back(attended)).reshape(-1, model_width)
    after_attention = inputs + low_back(jnp.dot(mixed, out_weight, precision=HIGHEST)).reshape(inputs.shape)
    flat_two = low(normalize(after_attention)[0] * feedforward_gain).reshape(-1, model_width)
    gate_lin = low_back(jnp.dot(flat_two, gate_weight, precision=HIGHEST))
    upward = low_back(jnp.dot(flat_two, up_weight, precision=HIGHEST))
    hidden = low(jax.nn.silu(gate_lin) * upward)
    branch = low_back(jnp.dot(hidden, down_weight, precision=HIGHEST))
    return after_attention + branch.reshape(inputs.shape)

def reference(layer_input, output_grad, doc_ids, keep_mask, attention_gain, query_weight, key_weight, value_weight, out_weight, feedforward_gain, gate_weight, up_weight, down_weight):
    floats = [operand.astype(jnp.float32) for operand in (layer_input, attention_gain, query_weight, key_weight, value_weight, out_weight, feedforward_gain, gate_weight, up_weight, down_weight)]

    def layer(*operands):
        return forward(*operands, doc_ids, keep_mask)
    result, pullback = jax.vjp(layer, *floats)
    gradients = pullback(output_grad.astype(jnp.float32))
    return (result.astype(jnp.bfloat16), gradients[0].astype(jnp.bfloat16), gradients[1], gradients[2], gradients[3], gradients[4], gradients[5], gradients[6], gradients[7], gradients[8], gradients[9])
```

```python
import functools

import jax
import jax.numpy as jnp
import numpy as np
from jax import lax
from jax.experimental import pallas as pl
from jax.experimental.pallas import tpu as pltpu
from jax.sharding import PartitionSpec as P

HEADS = 32
HEAD = 64
DOCS = 3
EPSILON = 1e-05
MASKED = -1e30
INNER = 2
F32 = jnp.float32
BF16 = jnp.bfloat16


def inverse_rates(head_width):
    plain = 500000.0 ** (-(np.arange(0, head_width, 2) * 1.0) / head_width)
    wavelength = 2.0 * np.pi / plain
    smooth = (8192.0 / wavelength - 1.0) / 3.0
    blended = (1.0 - smooth) * plain / 32.0 + smooth * plain
    scaled = np.where(
        wavelength > 8192.0, plain / 32.0, np.where(wavelength < 2048.0, plain, blended)
    )
    return scaled.astype(np.float32)


def stream_positions(documents):
    numbers = jnp.arange(DOCS, dtype=jnp.int32)
    starts = jnp.sum((documents[None, :] < numbers[:, None]).astype(jnp.int32), axis=1)
    own_start = jnp.sum(
        jnp.where(documents[:, None] == numbers[None, :], starts[None, :], 0), axis=1
    )
    return jnp.arange(documents.shape[0], dtype=jnp.int32) - own_start


def normalize(values):
    factor = lax.rsqrt(jnp.mean(values * values, axis=-1, keepdims=True) + EPSILON)
    return values * factor, factor


def mm(left, right, dims):
    return lax.dot_general(left, right, (dims, ((), ())), preferred_element_type=F32)


def block_offset(place, block, outer, tokens):
    peer = place ^ block
    return pl.multiple_of(((peer % INNER) * outer + peer // INNER) * tokens, tokens)


def fill_bias(bias_ref, keydoc_ref, doc_ref, start, width, length):
    shape = (length, width)
    key_index = lax.broadcasted_iota(jnp.int32, shape, 0)
    query_index = lax.broadcasted_iota(jnp.int32, shape, 1) + start
    allowed = (keydoc_ref[0:length, :] == doc_ref[:, start : start + width]) & (
        key_index <= query_index
    )
    bias_ref[0:length, :] = jnp.where(allowed, 0.0, MASKED)


def attend_kernel(
    heads, tokens, outer, width,
    place_ref, lin_ref, cos_ref, sin_ref, keydoc_ref, doc_ref,
    mixed_ref, query_ref, key_ref, value_ref, lse_ref,
    key_rows, bias_ref,
):
    length = doc_ref.shape[1]
    key_heads = key_ref.shape[0]
    group = heads // key_heads
    half = HEAD // 2
    place = place_ref[0]
    for block in range(length // tokens):
        source = pl.ds(block_offset(place, block, outer, tokens), tokens)
        lanes = slice(block * tokens, (block + 1) * tokens)
        cosine, sine = cos_ref[:, lanes], sin_ref[:, lanes]
        for head in range(heads + key_heads):
            first = lin_ref[head, 0:half, source]
            second = lin_ref[head, half:HEAD, source]
            one = (first * cosine - second * sine).astype(BF16)
            two = (second * cosine + first * sine).astype(BF16)
            if head < heads:
                scale = jnp.asarray(HEAD ** (-0.5), BF16)
                query_ref[head, 0:half, lanes] = one * scale
                query_ref[head, half:HEAD, lanes] = two * scale
            else:
                key_ref[head - heads, 0:half, lanes] = one
                key_ref[head - heads, half:HEAD, lanes] = two
        for head in range(key_heads):
            value_ref[head, :, lanes] = lin_ref[heads + key_heads + head, :, source].astype(BF16)
    for kv in range(key_heads):
        key_rows[kv] = key_ref[kv].astype(F32).T.astype(BF16)
    for step in range(length // width):
        start = step * width
        reach = start + width
        fill_bias(bias_ref, keydoc_ref, doc_ref, start, width, reach)
        for kv in range(key_heads):

            def one_head(index, carry, kv=kv, start=start, reach=reach):
                head = kv * group + index
                query = query_ref[head, :, start:reach]
                scores = mm(key_rows[kv, 0:reach, :], query, ((1,), (0,))) + bias_ref[0:reach, :]
                top = jnp.max(scores, axis=0, keepdims=True)
                terms = jnp.exp(scores - top)
                total = jnp.sum(terms, axis=0, keepdims=True)
                probs = (terms * (1.0 / total)).astype(BF16)
                mixed = mm(value_ref[kv, :, 0:reach], probs, ((1,), (0,))).astype(BF16)
                for block in range(start // tokens, reach // tokens):
                    target = pl.ds(block_offset(place, block, outer, tokens), tokens)
                    lanes = slice(block * tokens - start, (block + 1) * tokens - start)
                    mixed_ref[head, :, target] = mixed[:, lanes]
                lse_ref[head, :, start:reach] = top + jnp.log(total)
                return carry

            lax.fori_loop(0, group, one_head, 0)


def attend_back_kernel(
    heads, tokens, outer, width,
    place_ref, grad_ref, query_ref, key_ref, value_ref, lse_ref, cos_ref, sin_ref,
    keydoc_ref, doc_ref,
    out_ref,
    key_rows, value_rows, key_grad, value_grad, grad_abs, bias_ref,
):
    length = doc_ref.shape[1]
    key_heads = key_ref.shape[0]
    group = heads // key_heads
    half = HEAD // 2
    scale = HEAD ** (-0.5)
    place = place_ref[0]

    def put_back(head, block, gradient):
        target = pl.ds(block_offset(place, block, outer, tokens), tokens)
        lanes = slice(block * tokens, (block + 1) * tokens)
        cosine, sine = cos_ref[:, lanes], sin_ref[:, lanes]
        one, two = gradient[0:half], gradient[half:HEAD]
        out_ref[head, 0:half, target] = (one * cosine + two * sine).astype(BF16)
        out_ref[head, half:HEAD, target] = (two * cosine - one * sine).astype(BF16)

    for block in range(length // tokens):
        source = pl.ds(block_offset(place, block, outer, tokens), tokens)
        lanes = slice(block * tokens, (block + 1) * tokens)
        for head in range(heads):
            grad_abs[head, :, lanes] = grad_ref[head, :, source]
    for kv in range(key_heads):
        key_rows[kv] = key_ref[kv].astype(F32).T.astype(BF16)
        value_rows[kv] = value_ref[kv].astype(F32).T.astype(BF16)
    key_grad[...] = jnp.zeros_like(key_grad)
    value_grad[...] = jnp.zeros_like(value_grad)
    for step in range(length // width):
        start = step * width
        reach = start + width
        fill_bias(bias_ref, keydoc_ref, doc_ref, start, width, reach)
        for kv in range(key_heads):

            def one_head(index, carry, kv=kv, start=start, reach=reach):
                head = kv * group + index
                query = query_ref[head, :, start:reach]
                grad = grad_abs[head, :, start:reach]
                query_rows = query.astype(F32).T.astype(BF16)
                grad_rows = grad.astype(F32).T.astype(BF16)
                scores = mm(key_rows[kv, 0:reach, :], query, ((1,), (0,))) + bias_ref[0:reach, :]
                probs = jnp.exp(scores - lse_ref[head, :, start:reach])
                grad_probs = mm(value_rows[kv, 0:reach, :], grad, ((1,), (0,)))
                delta = jnp.sum(probs * grad_probs, axis=0, keepdims=True)
                grad_scores = (probs * (grad_probs - delta)).astype(BF16)
                value_grad[kv, 0:reach, :] += mm(probs.astype(BF16), grad_rows, ((1,), (0,)))
                key_grad[kv, 0:reach, :] += mm(grad_scores, query_rows, ((1,), (0,)))
                grad_query = mm(key_ref[kv, :, 0:reach], grad_scores, ((1,), (0,))) * scale
                for block in range(start // tokens, reach // tokens):
                    lanes = slice(block * tokens - start, (block + 1) * tokens - start)
                    put_back(head, block, grad_query[:, lanes])
                return carry

            lax.fori_loop(0, group, one_head, 0)
    for block in range(length // tokens):
        lanes = slice(block * tokens, (block + 1) * tokens)
        target = pl.ds(block_offset(place, block, outer, tokens), tokens)
        for kv in range(key_heads):
            put_back(heads + kv, block, key_grad[kv, lanes, :].T)
            out_ref[heads + key_heads + kv, :, target] = value_grad[kv, lanes, :].T.astype(BF16)


def vmem_spec():
    return pl.BlockSpec(memory_space=pltpu.VMEM)


def attend(place, lin, cosine, sine, keydoc, doc, heads, tokens, outer):
    total, _, length = lin.shape
    key_heads = (total - heads) // 2
    width = min(256, length)
    shape = jax.ShapeDtypeStruct
    return pl.pallas_call(
        functools.partial(attend_kernel, heads, tokens, outer, width),
        out_shape=(
            shape((heads, HEAD, length), BF16),
            shape((heads, HEAD, length), BF16),
            shape((key_heads, HEAD, length), BF16),
            shape((key_heads, HEAD, length), BF16),
            shape((heads, 1, length), F32),
        ),
        in_specs=[pl.BlockSpec(memory_space=pltpu.SMEM)] + [vmem_spec()] * 5,
        out_specs=(vmem_spec(),) * 5,
        scratch_shapes=[
            pltpu.VMEM((key_heads, length, HEAD), BF16),
            pltpu.VMEM((length, width), F32),
        ],
        compiler_params=pltpu.CompilerParams(vmem_limit_bytes=40 * 2**20),
        cost_estimate=pl.CostEstimate(
            flops=4 * heads * length * length * HEAD,
            bytes_accessed=8 * total * HEAD * length,
            transcendentals=heads * length * length,
        ),
    )(place, lin, cosine, sine, keydoc, doc)


def attend_back(place, grad, query, key, value, lse, cosine, sine, keydoc, doc, tokens, outer):
    heads, _, length = query.shape
    key_heads = key.shape[0]
    width = min(256, length)
    total = heads + 2 * key_heads
    return pl.pallas_call(
        functools.partial(attend_back_kernel, heads, tokens, outer, width),
        out_shape=jax.ShapeDtypeStruct((total, HEAD, length), BF16),
        in_specs=[pl.BlockSpec(memory_space=pltpu.SMEM)] + [vmem_spec()] * 9,
        out_specs=vmem_spec(),
        scratch_shapes=[
            pltpu.VMEM((key_heads, length, HEAD), BF16),
            pltpu.VMEM((key_heads, length, HEAD), BF16),
            pltpu.VMEM((key_heads, length, HEAD), F32),
            pltpu.VMEM((key_heads, length, HEAD), F32),
            pltpu.VMEM((heads, HEAD, length), BF16),
            pltpu.VMEM((length, width), F32),
        ],
        compiler_params=pltpu.CompilerParams(vmem_limit_bytes=40 * 2**20),
        cost_estimate=pl.CostEstimate(
            flops=10 * heads * length * length * HEAD,
            bytes_accessed=8 * total * HEAD * length,
            transcendentals=heads * length * length,
        ),
    )(place, grad, query, key, value, lse, cosine, sine, keydoc, doc)


def exchange(value, axis, size, step):
    return lax.ppermute(value, axis, [(i, i ^ step) for i in range(size)])


def put(buffer, piece, index):
    return lax.dynamic_update_slice(
        buffer, piece, tuple(jnp.asarray(i, jnp.int32) for i in index)
    )


def pick(value, index, axis=0):
    return lax.dynamic_index_in_dim(value, index, axis, keepdims=False)


def make_program(wide, narrow):
    outer = wide // INNER

    def core_swap(value):
        return exchange(value, "wide", wide, 1)

    def outer_swap(value, step):
        return exchange(value, "wide", wide, INNER * step)

    def narrow_swap(value, step):
        return exchange(value, "narrow", narrow, step)

    def fan_out(value, swap, size):
        return [value] + [swap(value, step) for step in range(1, size)]

    def sum_scatter(parts, swap, size):
        arrived = [swap(parts[step].astype(BF16), step) for step in range(1, size)]
        total = parts[0].astype(F32)
        for piece in arrived:
            total = total + piece.astype(F32)
        return total

    def gather_near(value, swap, size):
        first = jnp.stack(fan_out(value, swap, size))
        return jnp.concatenate([first, core_swap(first)], axis=0).reshape(-1, value.shape[-1])

    def scatter_near(total, swap, size):
        split = total.reshape(INNER, size, -1, total.shape[-1])
        arrived = core_swap(split[1].astype(BF16))
        both = [split[0, step].astype(F32) + arrived[step].astype(F32) for step in range(size)]
        return sum_scatter(both, swap, size)

    def per_device(
        layer_input, output_grad, doc_ids, keep_mask, attention_gain, query_weight, key_weight,
        value_weight, out_weight, feedforward_gain, gate_weight, up_weight, down_weight,
    ):
        tokens = layer_input.shape[1]
        model = layer_input.shape[2]
        rows = query_weight.shape[0]
        down_rows = down_weight.shape[0]
        kv_total = key_weight.shape[1] // HEAD
        heads = HEADS // wide
        group = HEADS // kv_total
        key_heads = max(1, heads // group)
        repeat = max(1, group // heads)
        place = lax.axis_index("wide")
        core = place % INNER
        chip = place // INNER
        layer = lax.axis_index("narrow")
        place_arg = place.reshape(1).astype(jnp.int32)
        documents = doc_ids[0]
        positions = stream_positions(documents)
        angles = jnp.asarray(inverse_rates(HEAD))[:, None] * positions.astype(F32)[None, :]
        cosine, sine = jnp.cos(angles), jnp.sin(angles)
        keydoc = jnp.where(keep_mask[0] > 0, documents, -1)[:, None]
        doc = documents[None, :]

        head_cols = heads * HEAD
        kv_cols = key_heads * HEAD

        def kv_split(weight):
            parts = weight.reshape(rows, -1, kv_cols)
            return jnp.repeat(parts, repeat, axis=1)

        packed = jnp.concatenate(
            [query_weight.reshape(rows, wide, head_cols), kv_split(key_weight), kv_split(value_weight)],
            axis=2,
        )
        cols = packed.shape[2]
        packed = packed.reshape(rows, outer, INNER, cols).transpose(2, 1, 0, 3)
        mine = pick(packed, core)
        other = core_swap(pick(packed, 1 - core))
        pair = jnp.stack([mine, other], axis=1)
        blocks = [pick(pair, chip)] + [
            outer_swap(pick(pair, chip ^ step), step) for step in range(1, outer)
        ]
        by_wide = jnp.zeros((wide, 1, rows, cols), BF16)
        for step in range(outer):
            for near in range(INNER):
                by_wide = put(
                    by_wide, blocks[step][near][None, None], (place ^ (INNER * step + near), 0, 0, 0)
                )
        by_wide = by_wide.reshape(wide, rows, cols)
        attention_weight = jnp.zeros((wide, narrow, rows, cols), BF16)
        for step, piece in enumerate(fan_out(by_wide, narrow_swap, narrow)):
            attention_weight = put(attention_weight, piece[:, None], (0, layer ^ step, 0, 0))
        attention_weight = attention_weight.reshape(model, cols)

        out_own = jnp.zeros((narrow, rows, model), BF16)
        for step, piece in enumerate(fan_out(out_weight, narrow_swap, narrow)):
            out_own = put(out_own, piece[None], (layer ^ step, 0, 0))
        out_own = out_own.reshape(narrow * rows, model)

        gains = jnp.stack([attention_gain, feedforward_gain]).astype(F32)
        gain_buffer = jnp.zeros((2, wide, narrow, rows), F32)
        near_gains = jnp.stack([gains, core_swap(gains)])
        wide_gains = [near_gains] + [outer_swap(near_gains, s) for s in range(1, outer)]
        wide_gains = jnp.stack(wide_gains)
        for far in range(narrow):
            piece = wide_gains if far == 0 else narrow_swap(wide_gains, far)
            for step in range(outer):
                for near in range(INNER):
                    gain_buffer = put(
                        gain_buffer,
                        piece[step, near][:, None, None, :],
                        (0, place ^ (INNER * step + near), layer ^ far, 0),
                    )
        gain_one, gain_two = gain_buffer[0].reshape(1, model), gain_buffer[1].reshape(1, model)

        own_input = layer_input[0]
        residual = own_input.astype(F32)
        all_input = gather_near(own_input, outer_swap, outer)
        normed_one = (normalize(all_input.astype(F32))[0] * gain_one).astype(BF16)
        lin = mm(attention_weight, normed_one, ((0,), (1,)))
        lin = lin.reshape(-1, HEAD, lin.shape[1])
        mixed, query, key, value, lse = attend(
            place_arg, lin, cosine, sine, keydoc, doc, heads, tokens, outer
        )
        mixed = mixed.reshape(head_cols, -1)
        attended = scatter_near(mm(mixed, out_own, ((0,), (0,))), outer_swap, outer)
        after_attention = residual + attended
        scaled_two, factor_two = normalize(after_attention)
        normed_own = (scaled_two * gain_two).astype(BF16)

        def for_group(weight):
            return weight.reshape(rows, outer, INNER, narrow, down_rows)

        pair_weight = jnp.stack([for_group(gate_weight), for_group(up_weight)])
        pair_weight = pair_weight.transpose(3, 4, 1, 0, 2, 5)
        pair_cols = 2 * outer * down_rows
        pair_weight = pair_weight.reshape(INNER, narrow, rows, pair_cols)
        mine = pick(pair_weight, core)
        other = core_swap(pick(pair_weight, 1 - core))
        near_pair = jnp.stack([mine, other])
        column = jnp.zeros((INNER, narrow, rows, pair_cols), BF16)
        for step in range(narrow):
            piece = pick(near_pair, layer ^ step, 1)
            if step:
                piece = narrow_swap(piece, step)
            for near in range(INNER):
                column = put(column, piece[near][None, None], (core ^ near, layer ^ step, 0, 0))
        gate_up = jnp.zeros((outer, INNER * narrow * rows, pair_cols), BF16)
        column = column.reshape(INNER * narrow * rows, pair_cols)
        for step, piece in enumerate(fan_out(column, outer_swap, outer)):
            gate_up = put(gate_up, piece[None], (chip ^ step, 0, 0))
        gate_up = gate_up.reshape(model, pair_cols)
        down = jnp.zeros((outer, down_rows, model), BF16)
        for step, piece in enumerate(fan_out(down_weight, outer_swap, outer)):
            down = put(down, piece[None], (chip ^ step, 0, 0))
        down = down.reshape(outer * down_rows, model)

        grad_out_own = output_grad[0]
        grad_out = gather_near(grad_out_own, narrow_swap, narrow)
        normed_two = gather_near(normed_own, narrow_swap, narrow)
        both = mm(normed_two, gate_up, ((1,), (0,)))
        units = pair_cols // 2
        gate, upward = both[:, :units], both[:, units:]
        sigmoid_gate = jax.nn.sigmoid(gate)
        activated = gate * sigmoid_gate
        hidden = (activated * upward).astype(BF16)
        grad_hidden = mm(grad_out, down, ((1,), (1,)))
        slope = sigmoid_gate * (1.0 + gate * (1.0 - sigmoid_gate))
        grad_gate = (grad_hidden * upward * slope).astype(BF16)
        grad_up = (grad_hidden * activated).astype(BF16)
        grad_pair = jnp.concatenate([grad_gate, grad_up], axis=1)
        grad_two = scatter_near(mm(grad_pair, gate_up, ((1,), (1,))), narrow_swap, narrow)

        grad_scaled_two = grad_two * gain_two
        grad_middle = grad_out_own.astype(F32) + factor_two * (
            grad_scaled_two
            - scaled_two * jnp.mean(grad_scaled_two * scaled_two, axis=-1, keepdims=True)
        )
        grad_attention = gather_near(grad_middle.astype(BF16), outer_swap, outer)
        grad_mixed = mm(out_own, grad_attention, ((1,), (1,))).astype(BF16)
        grad_lin = attend_back(
            place_arg, grad_mixed.reshape(heads, HEAD, -1), query, key, value, lse, cosine, sine,
            keydoc, doc, tokens, outer,
        ).reshape(cols, -1)
        grad_one = scatter_near(mm(grad_lin, attention_weight, ((0,), (1,))), outer_swap, outer)
        scaled_one, factor_one = normalize(residual)
        grad_scaled_one = grad_one * gain_one
        input_grad = grad_middle + factor_one * (
            grad_scaled_one
            - scaled_one * jnp.mean(grad_scaled_one * scaled_one, axis=-1, keepdims=True)
        )

        branch = scatter_near(mm(hidden, down, ((1,), (0,))), narrow_swap, narrow)
        layer_output = after_attention + branch

        down_term = mm(hidden, grad_out, ((0,), (0,))).reshape(outer, down_rows, model)
        down_grad = sum_scatter(
            [pick(down_term, chip ^ step) for step in range(outer)], outer_swap, outer
        )
        pair_term = mm(normed_two, grad_pair, ((0,), (0,))).reshape(outer, -1, pair_cols)
        pair_sum = sum_scatter(
            [pick(pair_term, chip ^ step) for step in range(outer)], outer_swap, outer
        )
        pair_sum = pair_sum.astype(BF16).reshape(INNER, narrow, rows, pair_cols)
        mine = pick(pair_sum, core)
        other = core_swap(pick(pair_sum, 1 - core))
        near_pair = jnp.stack([mine, other])
        pair_grad = jnp.zeros((2, rows, outer, INNER, narrow, down_rows), F32)
        for step in range(narrow):
            piece = pick(near_pair, layer ^ step, 1)
            if step:
                piece = narrow_swap(piece, step)
            piece = piece.astype(F32).reshape(INNER, rows, 2, outer, down_rows)
            piece = piece.transpose(0, 2, 1, 3, 4)
            for near in range(INNER):
                pair_grad = put(
                    pair_grad,
                    piece[near][:, :, :, None, None, :],
                    (0, 0, 0, core ^ near, layer ^ step, 0),
                )
        pair_grad = pair_grad.reshape(2, rows, -1)
        gate_grad, up_grad = pair_grad[0], pair_grad[1]
        gain_two_grad = (
            jnp.sum(gate_grad * gate_weight.astype(F32), axis=1)
            + jnp.sum(up_grad * up_weight.astype(F32), axis=1)
        ) / feedforward_gain.astype(F32)

        out_term = mm(mixed, grad_attention, ((1,), (0,))).reshape(narrow, rows, model)
        out_grad = sum_scatter(
            [pick(out_term, layer ^ step) for step in range(narrow)], narrow_swap, narrow
        )
        lin_term = mm(normed_one, grad_lin, ((0,), (1,))).reshape(wide, narrow, rows, cols)
        lin_sum = sum_scatter(
            [pick(lin_term, layer ^ step, 1) for step in range(narrow)], narrow_swap, narrow
        )
        lin_sum = lin_sum.astype(BF16).reshape(outer, INNER, rows, cols)
        mine = pick(lin_sum, core, 1)
        other = core_swap(pick(lin_sum, 1 - core, 1))
        pair = jnp.stack([mine, other], axis=1)
        lin_grad = jnp.zeros((wide, rows, cols), F32)
        for step in range(outer):
            piece = pick(pair, chip ^ step)
            if step:
                piece = outer_swap(piece, step)
            for near in range(INNER):
                lin_grad = put(
                    lin_grad, piece[near][None].astype(F32), (place ^ (INNER * step + near), 0, 0)
                )
        query_grad = lin_grad[:, :, :head_cols].transpose(1, 0, 2).reshape(rows, -1)

        def kv_join(part):
            joined = part.reshape(wide // repeat, repeat, rows, kv_cols).sum(axis=1)
            return joined.transpose(1, 0, 2).reshape(rows, -1)

        key_grad = kv_join(lin_grad[:, :, head_cols : head_cols + kv_cols])
        value_grad = kv_join(lin_grad[:, :, head_cols + kv_cols :])
        gain_one_grad = (
            jnp.sum(query_grad * query_weight.astype(F32), axis=1)
            + jnp.sum(key_grad * key_weight.astype(F32), axis=1)
            + jnp.sum(value_grad * value_weight.astype(F32), axis=1)
        ) / attention_gain.astype(F32)
        return (
            layer_output[None].astype(BF16),
            input_grad[None].astype(BF16),
            gain_one_grad,
            query_grad,
            key_grad,
            value_grad,
            out_grad,
            gain_two_grad,
            gate_grad,
            up_grad,
            down_grad,
        )

    return per_device


def solution(mesh):
    rows = P(("wide", "narrow"), None)
    line = P(("wide", "narrow"))
    stream = P("narrow", "wide", None)
    return jax.shard_map(
        make_program(mesh.shape["wide"], mesh.shape["narrow"]),
        mesh=mesh,
        in_specs=(
            stream, stream, P("narrow", None), P("narrow", None),
            line, rows, rows, rows, rows, line, rows, rows, rows,
        ),
        out_specs=(stream, stream, line, rows, rows, rows, rows, line, rows, rows, rows),
        check_vma=False,
    )
```

```python
import functools

import jax
import jax.numpy as jnp
import numpy as np
from jax import lax
from jax.experimental import pallas as pl
from jax.experimental.pallas import tpu as pltpu
from jax.sharding import PartitionSpec as P

HEADS = 32
HEAD = 64
DOCS = 3
EPSILON = 1e-05
MASKED = -1e30
INNER = 2
F32 = jnp.float32
BF16 = jnp.bfloat16


def inverse_rates(head_width):
    plain = 500000.0 ** (-(np.arange(0, head_width, 2) * 1.0) / head_width)
    wavelength = 2.0 * np.pi / plain
    smooth = (8192.0 / wavelength - 1.0) / 3.0
    blended = (1.0 - smooth) * plain / 32.0 + smooth * plain
    scaled = np.where(
        wavelength > 8192.0, plain / 32.0, np.where(wavelength < 2048.0, plain, blended)
    )
    return scaled.astype(np.float32)


def stream_positions(documents):
    numbers = jnp.arange(DOCS, dtype=jnp.int32)
    starts = jnp.sum((documents[None, :] < numbers[:, None]).astype(jnp.int32), axis=1)
    own_start = jnp.sum(
        jnp.where(documents[:, None] == numbers[None, :], starts[None, :], 0), axis=1
    )
    return jnp.arange(documents.shape[0], dtype=jnp.int32) - own_start


def normalize(values):
    factor = lax.rsqrt(jnp.mean(values * values, axis=-1, keepdims=True) + EPSILON)
    return values * factor, factor


def mm(left, right, dims):
    return lax.dot_general(left, right, (dims, ((), ())), preferred_element_type=F32)


def block_offset(place, block, outer, tokens):
    peer = place ^ block
    return pl.multiple_of(((peer % INNER) * outer + peer // INNER) * tokens, tokens)


def fill_bias(bias_ref, keydoc_ref, doc_ref, start, width, length):
    shape = (length, width)
    key_index = lax.broadcasted_iota(jnp.int32, shape, 0)
    query_index = lax.broadcasted_iota(jnp.int32, shape, 1) + start
    allowed = (keydoc_ref[0:length, :] == doc_ref[:, start : start + width]) & (
        key_index <= query_index
    )
    bias_ref[0:length, :] = jnp.where(allowed, 0.0, MASKED)


def attend_kernel(
    heads, tokens, outer, width,
    place_ref, lin_ref, cos_ref, sin_ref, keydoc_ref, doc_ref,
    mixed_ref, query_ref, key_ref, value_ref, lse_ref,
    key_rows, bias_ref,
):
    length = doc_ref.shape[1]
    key_heads = key_ref.shape[0]
    group = heads // key_heads
    half = HEAD // 2
    place = place_ref[0]
    for block in range(length // tokens):
        source = pl.ds(block_offset(place, block, outer, tokens), tokens)
        lanes = slice(block * tokens, (block + 1) * tokens)
        cosine, sine = cos_ref[:, lanes], sin_ref[:, lanes]
        for head in range(heads + key_heads):
            first = lin_ref[head, 0:half, source]
            second = lin_ref[head, half:HEAD, source]
            one = (first * cosine - second * sine).astype(BF16)
            two = (second * cosine + first * sine).astype(BF16)
            if head < heads:
                scale = jnp.asarray(HEAD ** (-0.5), BF16)
                query_ref[head, 0:half, lanes] = one * scale
                query_ref[head, half:HEAD, lanes] = two * scale
            else:
                key_ref[head - heads, 0:half, lanes] = one
                key_ref[head - heads, half:HEAD, lanes] = two
        for head in range(key_heads):
            value_ref[head, :, lanes] = lin_ref[heads + key_heads + head, :, source].astype(BF16)
    for kv in range(key_heads):
        key_rows[kv] = key_ref[kv].astype(F32).T.astype(BF16)
    for step in range(length // width):
        start = step * width
        reach = start + width
        fill_bias(bias_ref, keydoc_ref, doc_ref, start, width, reach)
        for kv in range(key_heads):

            def one_head(index, carry, kv=kv, start=start, reach=reach):
                head = kv * group + index
                query = query_ref[head, :, start:reach]
                scores = mm(key_rows[kv, 0:reach, :], query, ((1,), (0,))) + bias_ref[0:reach, :]
                top = jnp.max(scores, axis=0, keepdims=True)
                terms = jnp.exp(scores - top)
                total = jnp.sum(terms, axis=0, keepdims=True)
                probs = (terms * (1.0 / total)).astype(BF16)
                mixed = mm(value_ref[kv, :, 0:reach], probs, ((1,), (0,))).astype(BF16)
                for block in range(start // tokens, reach // tokens):
                    target = pl.ds(block_offset(place, block, outer, tokens), tokens)
                    lanes = slice(block * tokens - start, (block + 1) * tokens - start)
                    mixed_ref[head, :, target] = mixed[:, lanes]
                lse_ref[head, :, start:reach] = top + jnp.log(total)
                return carry

            lax.fori_loop(0, group, one_head, 0)


def attend_back_kernel(
    heads, tokens, outer, width,
    place_ref, grad_ref, query_ref, key_ref, value_ref, lse_ref, cos_ref, sin_ref,
    keydoc_ref, doc_ref,
    out_ref,
    key_rows, value_rows, key_grad, value_grad, grad_abs, bias_ref,
):
    length = doc_ref.shape[1]
    key_heads = key_ref.shape[0]
    group = heads // key_heads
    half = HEAD // 2
    scale = HEAD ** (-0.5)
    place = place_ref[0]

    def put_back(head, block, gradient):
        target = pl.ds(block_offset(place, block, outer, tokens), tokens)
        lanes = slice(block * tokens, (block + 1) * tokens)
        cosine, sine = cos_ref[:, lanes], sin_ref[:, lanes]
        one, two = gradient[0:half], gradient[half:HEAD]
        out_ref[head, 0:half, target] = (one * cosine + two * sine).astype(BF16)
        out_ref[head, half:HEAD, target] = (two * cosine - one * sine).astype(BF16)

    for block in range(length // tokens):
        source = pl.ds(block_offset(place, block, outer, tokens), tokens)
        lanes = slice(block * tokens, (block + 1) * tokens)
        for head in range(heads):
            grad_abs[head, :, lanes] = grad_ref[head, :, source]
    for kv in range(key_heads):
        key_rows[kv] = key_ref[kv].astype(F32).T.astype(BF16)
        value_rows[kv] = value_ref[kv].astype(F32).T.astype(BF16)
    key_grad[...] = jnp.zeros_like(key_grad)
    value_grad[...] = jnp.zeros_like(value_grad)
    for step in range(length // width):
        start = step * width
        reach = start + width
        fill_bias(bias_ref, keydoc_ref, doc_ref, start, width, reach)
        for kv in range(key_heads):

            def one_head(index, carry, kv=kv, start=start, reach=reach):
                head = kv * group + index
                query = query_ref[head, :, start:reach]
                grad = grad_abs[head, :, start:reach]
                query_rows = query.astype(F32).T.astype(BF16)
                grad_rows = grad.astype(F32).T.astype(BF16)
                scores = mm(key_rows[kv, 0:reach, :], query, ((1,), (0,))) + bias_ref[0:reach, :]
                probs = jnp.exp(scores - lse_ref[head, :, start:reach])
                grad_probs = mm(value_rows[kv, 0:reach, :], grad, ((1,), (0,)))
                delta = jnp.sum(probs * grad_probs, axis=0, keepdims=True)
                grad_scores = (probs * (grad_probs - delta)).astype(BF16)
                value_grad[kv, 0:reach, :] += mm(probs.astype(BF16), grad_rows, ((1,), (0,)))
                key_grad[kv, 0:reach, :] += mm(grad_scores, query_rows, ((1,), (0,)))
                grad_query = mm(key_ref[kv, :, 0:reach], grad_scores, ((1,), (0,))) * scale
                for block in range(start // tokens, reach // tokens):
                    lanes = slice(block * tokens - start, (block + 1) * tokens - start)
                    put_back(head, block, grad_query[:, lanes])
                return carry

            lax.fori_loop(0, group, one_head, 0)
    for block in range(length // tokens):
        lanes = slice(block * tokens, (block + 1) * tokens)
        target = pl.ds(block_offset(place, block, outer, tokens), tokens)
        for kv in range(key_heads):
            put_back(heads + kv, block, key_grad[kv, lanes, :].T)
            out_ref[heads + key_heads + kv, :, target] = value_grad[kv, lanes, :].T.astype(BF16)


def vmem_spec():
    return pl.BlockSpec(memory_space=pltpu.VMEM)


def attend(place, lin, cosine, sine, keydoc, doc, heads, tokens, outer):
    total, _, length = lin.shape
    key_heads = (total - heads) // 2
    width = min(256, length)
    shape = jax.ShapeDtypeStruct
    return pl.pallas_call(
        functools.partial(attend_kernel, heads, tokens, outer, width),
        out_shape=(
            shape((heads, HEAD, length), BF16),
            shape((heads, HEAD, length), BF16),
            shape((key_heads, HEAD, length), BF16),
            shape((key_heads, HEAD, length), BF16),
            shape((heads, 1, length), F32),
        ),
        in_specs=[pl.BlockSpec(memory_space=pltpu.SMEM)] + [vmem_spec()] * 5,
        out_specs=(vmem_spec(),) * 5,
        scratch_shapes=[
            pltpu.VMEM((key_heads, length, HEAD), BF16),
            pltpu.VMEM((length, width), F32),
        ],
        compiler_params=pltpu.CompilerParams(vmem_limit_bytes=40 * 2**20),
        cost_estimate=pl.CostEstimate(
            flops=4 * heads * length * length * HEAD,
            bytes_accessed=8 * total * HEAD * length,
            transcendentals=heads * length * length,
        ),
    )(place, lin, cosine, sine, keydoc, doc)


def attend_back(place, grad, query, key, value, lse, cosine, sine, keydoc, doc, tokens, outer):
    heads, _, length = query.shape
    key_heads = key.shape[0]
    width = min(256, length)
    total = heads + 2 * key_heads
    return pl.pallas_call(
        functools.partial(attend_back_kernel, heads, tokens, outer, width),
        out_shape=jax.ShapeDtypeStruct((total, HEAD, length), BF16),
        in_specs=[pl.BlockSpec(memory_space=pltpu.SMEM)] + [vmem_spec()] * 9,
        out_specs=vmem_spec(),
        scratch_shapes=[
            pltpu.VMEM((key_heads, length, HEAD), BF16),
            pltpu.VMEM((key_heads, length, HEAD), BF16),
            pltpu.VMEM((key_heads, length, HEAD), F32),
            pltpu.VMEM((key_heads, length, HEAD), F32),
            pltpu.VMEM((heads, HEAD, length), BF16),
            pltpu.VMEM((length, width), F32),
        ],
        compiler_params=pltpu.CompilerParams(vmem_limit_bytes=40 * 2**20),
        cost_estimate=pl.CostEstimate(
            flops=10 * heads * length * length * HEAD,
            bytes_accessed=8 * total * HEAD * length,
            transcendentals=heads * length * length,
        ),
    )(place, grad, query, key, value, lse, cosine, sine, keydoc, doc)


def join_kernel(down_rows, gate_part, up_part, gate_weight, up_weight, gate_ref, up_ref, sum_ref):
    @pl.when(pl.program_id(0) == 0)
    def _():
        sum_ref[...] = jnp.zeros_like(sum_ref)

    for part, weight, out in ((gate_part, gate_weight, gate_ref), (up_part, up_weight, up_ref)):
        for block in range(part.shape[0]):
            lanes = slice(block * down_rows, (block + 1) * down_rows)
            piece = part[block].astype(F32)
            out[:, lanes] = piece
            term = piece * weight[:, lanes].astype(F32)
            sum_ref[...] += jnp.sum(term, axis=1, keepdims=True)


def join_pair(pair_grad, gate_weight, up_weight, outer, down_rows):
    blocks, rows, _ = pair_grad.shape
    units = gate_weight.shape[1]
    width = blocks * down_rows
    shape = jax.ShapeDtypeStruct
    wide_spec = pl.BlockSpec((rows, width), lambda i: (0, i))
    return pl.pallas_call(
        functools.partial(join_kernel, down_rows),
        grid=(outer,),
        out_shape=(
            shape((rows, units), F32), shape((rows, units), F32), shape((rows, 128), F32),
        ),
        in_specs=[
            pl.BlockSpec((blocks, rows, down_rows), lambda i: (0, 0, i)),
            pl.BlockSpec((blocks, rows, down_rows), lambda i: (0, 0, i + outer)),
            wide_spec,
            wide_spec,
        ],
        out_specs=(wide_spec, wide_spec, pl.BlockSpec((rows, 128), lambda i: (0, 0))),
        compiler_params=pltpu.CompilerParams(vmem_limit_bytes=32 * 2**20),
        cost_estimate=pl.CostEstimate(
            flops=4 * rows * units, bytes_accessed=16 * rows * units, transcendentals=0
        ),
    )(pair_grad, pair_grad, gate_weight, up_weight)


def exchange(value, axis, size, step):
    return lax.ppermute(value, axis, [(i, i ^ step) for i in range(size)])


def put(buffer, piece, index):
    return lax.dynamic_update_slice(
        buffer, piece, tuple(jnp.asarray(i, jnp.int32) for i in index)
    )


def pick(value, index, axis=0):
    return lax.dynamic_index_in_dim(value, index, axis, keepdims=False)


def after(value, *marks):
    return lax.optimization_barrier((value,) + marks)[0]


def make_program(wide, narrow):
    outer = wide // INNER
    near_size = INNER * narrow
    near_groups = [[o * near_size + i for i in range(near_size)] for o in range(outer)]
    chip_groups = [[c + INNER * o for o in range(outer)] for c in range(INNER)]
    both = ("wide", "narrow")

    def core_swap(value):
        return exchange(value, "wide", wide, 1)

    def outer_swap(value, step):
        return exchange(value, "wide", wide, INNER * step)

    def narrow_swap(value, step):
        return exchange(value, "narrow", narrow, step)

    def fan_out(value, swap, size):
        return [value] + [swap(value, step) for step in range(1, size)]

    def narrow_gather(value):
        spread = jnp.broadcast_to(value[None], (narrow,) + value.shape)
        return lax.all_to_all(spread, "narrow", 0, 0, tiled=True)

    def narrow_sum(total):
        split = total.reshape(narrow, -1, total.shape[-1])
        return lax.all_to_all(split, "narrow", 0, 0, tiled=True)

    def with_sibling(first):
        return jnp.concatenate([first, core_swap(first)], axis=0)

    def join_near(parts):
        first = jnp.concatenate(parts, axis=0)
        return jnp.concatenate([first, core_swap(first)], axis=0)

    def near_total(product):
        arrived = core_swap(product(1).astype(BF16))
        return (product(0) + arrived.astype(F32)).astype(BF16), arrived

    def scatter(total, swap, size):
        split = total.reshape(size, -1, total.shape[-1])
        return [split[0]] + [swap(split[step], step) for step in range(1, size)]

    def add_up(parts):
        total = parts[0].astype(F32)
        for piece in parts[1:]:
            total = total + piece.astype(F32)
        return total

    def per_device(
        layer_input, output_grad, doc_ids, keep_mask, attention_gain, query_weight, key_weight,
        value_weight, out_weight, feedforward_gain, gate_weight, up_weight, down_weight,
    ):
        tokens = layer_input.shape[1]
        model = layer_input.shape[2]
        rows = query_weight.shape[0]
        down_rows = down_weight.shape[0]
        kv_total = key_weight.shape[1] // HEAD
        heads = HEADS // wide
        group = HEADS // kv_total
        key_heads = max(1, heads // group)
        repeat = max(1, group // heads)
        place = lax.axis_index("wide")
        chip = place // INNER
        layer = lax.axis_index("narrow")
        core = place % INNER
        place_arg = place.reshape(1).astype(jnp.int32)

        head_cols = heads * HEAD
        kv_cols = key_heads * HEAD

        def kv_split(weight):
            parts = weight.reshape(rows, -1, kv_cols)
            return jnp.repeat(parts, repeat, axis=1)

        packed = jnp.concatenate(
            [query_weight.reshape(rows, wide, head_cols), kv_split(key_weight), kv_split(value_weight)],
            axis=2,
        )
        cols = packed.shape[2]
        own_input = layer_input[0]
        residual = own_input.astype(F32)
        out_parts = fan_out(out_weight, narrow_swap, narrow)
        packed = packed.transpose(1, 0, 2)
        gain_rows = -(-2 * rows // cols) * 8
        gains = jnp.concatenate([attention_gain, feedforward_gain])
        gains = jnp.pad(gains, (0, gain_rows * cols - 2 * rows)).reshape(1, gain_rows, cols)
        gains = jnp.broadcast_to(gains, (wide, gain_rows, cols))
        packed = jnp.concatenate([packed, gains], axis=1)
        by_wide = lax.all_to_all(packed, "wide", 0, 0, tiled=True)
        input_parts = fan_out(after(own_input, by_wide), outer_swap, outer)

        weight_parts = fan_out(after(by_wide, *out_parts), narrow_swap, narrow)

        def for_group(weight):
            return weight.reshape(rows, outer, near_size, down_rows).transpose(2, 0, 1, 3)

        pair_cols = 2 * outer * down_rows
        units = pair_cols // 2
        pair_weight = jnp.stack([for_group(gate_weight), for_group(up_weight)], axis=2)
        pair_weight = pair_weight.reshape(near_size, rows, pair_cols)
        pair_weight = after(pair_weight, *weight_parts, *input_parts)
        column = lax.all_to_all(
            pair_weight, both, 0, 0, axis_index_groups=near_groups, tiled=True
        )
        down = lax.all_gather(
            down_weight, "wide", axis=0, tiled=True, axis_index_groups=chip_groups
        )

        all_input = join_near(input_parts)
        scaled_all, factor_all = normalize(all_input.astype(F32))
        attention_weight = after(jnp.zeros((wide, narrow, rows, cols), BF16), factor_all)
        for step, piece in enumerate(weight_parts):
            attention_weight = put(
                attention_weight, piece[:, None, :rows], (0, layer ^ step, 0, 0)
            )
        attention_weight = attention_weight.reshape(model, cols)
        lines = jnp.stack([piece[:, rows, : 2 * rows] for piece in weight_parts], axis=1)
        lines = jnp.stack([pick(lines, layer ^ step, 1) for step in range(narrow)], axis=1)
        lines = lines.astype(F32)
        gain_one = lines[:, :, :rows].reshape(1, model)
        gain_two = lines[:, :, rows:].reshape(1, model)

        out_own = jnp.zeros((narrow, rows, model), BF16)
        for step, piece in enumerate(out_parts):
            out_own = put(out_own, piece[None], (layer ^ step, 0, 0))
        out_own = out_own.reshape(narrow * rows, model)

        grad_out_own = output_grad[0]
        grad_out_near = narrow_gather(after(grad_out_own, column)).reshape(-1, model)

        own = all_input.shape[0] // INNER
        half = near_size * tokens // INNER
        documents = doc_ids[0]
        positions = stream_positions(documents)
        angles = jnp.asarray(inverse_rates(HEAD))[:, None] * positions.astype(F32)[None, :]
        cosine, sine = jnp.cos(angles), jnp.sin(angles)
        keydoc = jnp.where(keep_mask[0] > 0, documents, -1)[:, None]
        doc = documents[None, :]
        normed_one = (scaled_all * gain_one).astype(BF16)
        lin = mm(attention_weight, normed_one, ((0,), (1,)))
        lin = lin.reshape(-1, HEAD, lin.shape[1])
        mixed, query, key, value, lse = attend(
            place_arg, lin, cosine, sine, keydoc, doc, heads, tokens, outer
        )
        mixed = mixed.reshape(head_cols, -1)

        def out_product(near):
            return mm(mixed[:, near * own : (near + 1) * own], out_own, ((0,), (0,)))

        attended, _ = near_total(out_product)
        gate_up = lax.all_gather(
            after(column.reshape(near_size * rows, pair_cols), down, attended), "wide", axis=0, tiled=True,
            axis_index_groups=chip_groups,
        )
        attended_parts = scatter(attended, outer_swap, outer)
        attended_parts[0] = after(attended_parts[0], grad_out_near)
        after_attention = residual + add_up(attended_parts)
        scaled_two, factor_two = normalize(after_attention)
        normed_own = (scaled_two * gain_two).astype(BF16)

        normed_near = narrow_gather(normed_own).reshape(-1, model)
        normed_two = with_sibling(normed_near)
        grad_out = with_sibling(grad_out_near)
        pair = mm(normed_two, gate_up, ((1,), (0,)))
        gate, upward = pair[:, :units], pair[:, units:]
        sigmoid_gate = jax.nn.sigmoid(gate)
        activated = gate * sigmoid_gate
        hidden = (activated * upward).astype(BF16)
        grad_hidden = mm(grad_out, down, ((1,), (1,)))
        slope = sigmoid_gate * (1.0 + gate * (1.0 - sigmoid_gate))
        grad_gate = (grad_hidden * upward * slope).astype(BF16)
        grad_up = (grad_hidden * activated).astype(BF16)
        grad_pair = jnp.concatenate([grad_gate, grad_up], axis=1)

        def two_product(near):
            return mm(grad_pair[near * half : (near + 1) * half], gate_up, ((1,), (1,)))

        two_total, _ = near_total(two_product)
        two_parts = narrow_sum(two_total)

        pair_term = mm(normed_two, after(grad_pair, two_total), ((0,), (0,))).astype(BF16)
        pair_sum = lax.psum_scatter(
            pair_term, "wide", scatter_dimension=0, tiled=True, axis_index_groups=chip_groups
        )
        late_hidden = after(hidden, pair_term)

        def branch_product(near):
            return mm(late_hidden[near * half : (near + 1) * half], down, ((1,), (0,)))

        branch_total, _ = near_total(branch_product)
        down_term = mm(late_hidden, grad_out, ((0,), (0,))).astype(BF16)
        grad_two = jnp.sum(after(two_parts, branch_total).astype(F32), axis=0)
        branch_parts = narrow_sum(after(branch_total, grad_two))
        layer_output = after_attention + jnp.sum(branch_parts.astype(F32), axis=0)
        down_grad = lax.psum_scatter(
            after(down_term, pair_sum), "wide", scatter_dimension=0, tiled=True,
            axis_index_groups=chip_groups,
        ).astype(F32)

        grad_scaled_two = grad_two * gain_two
        grad_middle = grad_out_own.astype(F32) + factor_two * (
            grad_scaled_two
            - scaled_two * jnp.mean(grad_scaled_two * scaled_two, axis=-1, keepdims=True)
        )
        middle_parts = fan_out(grad_middle.astype(BF16), outer_swap, outer)
        middle_parts[0] = after(middle_parts[0], down_term)
        grad_attention = join_near(middle_parts)
        grad_mixed = mm(out_own, grad_attention, ((1,), (1,)))
        grad_mixed = grad_mixed.astype(BF16)
        grad_lin = attend_back(
            place_arg, grad_mixed.reshape(heads, HEAD, -1), query, key, value, lse, cosine, sine,
            keydoc, doc, tokens, outer,
        ).reshape(cols, -1)

        def one_product(near):
            return mm(grad_lin[:, near * own : (near + 1) * own], attention_weight, ((0,), (1,)))

        one_total, one_swapped = near_total(one_product)
        grad_one = add_up(scatter(one_total, outer_swap, outer))
        scaled_one, factor_one = normalize(residual)
        grad_scaled_one = grad_one * gain_one
        input_grad = grad_middle + factor_one * (
            grad_scaled_one
            - scaled_one * jnp.mean(grad_scaled_one * scaled_one, axis=-1, keepdims=True)
        )

        pair_sum = after(pair_sum, branch_parts).reshape(near_size, rows, pair_cols)
        pair_grad = lax.all_to_all(pair_sum, both, 0, 0, axis_index_groups=near_groups, tiled=True)
        if down_rows % 128 == 0:
            gate_grad, up_grad, gain_sum = join_pair(
                pair_grad, gate_weight, up_weight, outer, down_rows
            )
            gain_sum = gain_sum[:, 0]
        else:
            pair_grad = pair_grad.reshape(near_size, rows, 2, outer, down_rows)
            pair_grad = pair_grad.transpose(2, 1, 3, 0, 4).reshape(2, rows, -1).astype(F32)
            gate_grad, up_grad = pair_grad[0], pair_grad[1]
            gain_sum = jnp.sum(gate_grad * gate_weight.astype(F32), axis=1) + jnp.sum(
                up_grad * up_weight.astype(F32), axis=1
            )
        gain_two_grad = gain_sum / feedforward_gain.astype(F32)

        late_lin = after(grad_lin, one_swapped)
        lin_term = mm(normed_one, late_lin, ((0,), (1,))).astype(BF16)
        lin_term = lin_term.reshape(wide, narrow, rows, cols).transpose(1, 0, 2, 3)
        lin_term = after(lin_term, pair_grad)
        lin_sum = jnp.sum(lax.all_to_all(lin_term, "narrow", 0, 0, tiled=True).astype(F32), axis=0)
        lin_grad = lax.all_to_all(lin_sum.astype(BF16), "wide", 0, 0, tiled=True).astype(F32)
        out_term = mm(mixed, after(grad_attention, late_lin), ((1,), (0,))).astype(BF16)
        out_term = out_term.reshape(narrow, rows, model)
        out_grad = jnp.sum(lax.all_to_all(out_term, "narrow", 0, 0, tiled=True).astype(F32), axis=0)

        query_grad = lin_grad[:, :, :head_cols].transpose(1, 0, 2).reshape(rows, -1)

        def kv_join(part):
            joined = part.reshape(wide // repeat, repeat, rows, kv_cols).sum(axis=1)
            return joined.transpose(1, 0, 2).reshape(rows, -1)

        key_grad = kv_join(lin_grad[:, :, head_cols : head_cols + kv_cols])
        value_grad = kv_join(lin_grad[:, :, head_cols + kv_cols :])
        gain_one_grad = (
            jnp.sum(query_grad * query_weight.astype(F32), axis=1)
            + jnp.sum(key_grad * key_weight.astype(F32), axis=1)
            + jnp.sum(value_grad * value_weight.astype(F32), axis=1)
        ) / attention_gain.astype(F32)
        return (
            layer_output[None].astype(BF16),
            input_grad[None].astype(BF16),
            gain_one_grad,
            query_grad,
            key_grad,
            value_grad,
            out_grad,
            gain_two_grad,
            gate_grad,
            up_grad,
            down_grad,
        )

    return per_device


def solution(mesh):
    rows = P(("wide", "narrow"), None)
    line = P(("wide", "narrow"))
    stream = P("narrow", "wide", None)
    return jax.shard_map(
        make_program(mesh.shape["wide"], mesh.shape["narrow"]),
        mesh=mesh,
        in_specs=(
            stream, stream, P("narrow", None), P("narrow", None),
            line, rows, rows, rows, rows, line, rows, rows, rows,
        ),
        out_specs=(stream, stream, line, rows, rows, rows, rows, line, rows, rows, rows),
        check_vma=False,
    )
```

```python
import functools

import jax
import jax.numpy as jnp
import numpy as np
from jax import lax
from jax.experimental import pallas as pl
from jax.experimental.pallas import tpu as pltpu
from jax.sharding import PartitionSpec as P

HEADS = 32
HEAD = 64
DOCS = 3
EPSILON = 1e-05
MASKED = -1e30
INNER = 2
HALVES = 2
F32 = jnp.float32
BF16 = jnp.bfloat16


def inverse_rates(head_width):
    plain = 500000.0 ** (-(np.arange(0, head_width, 2) * 1.0) / head_width)
    wavelength = 2.0 * np.pi / plain
    smooth = (8192.0 / wavelength - 1.0) / 3.0
    blended = (1.0 - smooth) * plain / 32.0 + smooth * plain
    scaled = np.where(
        wavelength > 8192.0, plain / 32.0, np.where(wavelength < 2048.0, plain, blended)
    )
    return scaled.astype(np.float32)


def stream_positions(documents):
    numbers = jnp.arange(DOCS, dtype=jnp.int32)
    starts = jnp.sum((documents[None, :] < numbers[:, None]).astype(jnp.int32), axis=1)
    own_start = jnp.sum(
        jnp.where(documents[:, None] == numbers[None, :], starts[None, :], 0), axis=1
    )
    return jnp.arange(documents.shape[0], dtype=jnp.int32) - own_start


def normalize(values):
    factor = lax.rsqrt(jnp.mean(values * values, axis=-1, keepdims=True) + EPSILON)
    return values * factor, factor


def mm(left, right, dims):
    return lax.dot_general(left, right, (dims, ((), ())), preferred_element_type=F32)


def block_offset(place, block, outer, tokens):
    peer = place ^ block
    return pl.multiple_of(((peer % INNER) * outer + peer // INNER) * tokens, tokens)


def fill_bias(bias_ref, keydoc_ref, doc_ref, start, width, length):
    shape = (length, width)
    key_index = lax.broadcasted_iota(jnp.int32, shape, 0)
    query_index = lax.broadcasted_iota(jnp.int32, shape, 1) + start
    allowed = (keydoc_ref[0:length, :] == doc_ref[:, start : start + width]) & (
        key_index <= query_index
    )
    bias_ref[0:length, :] = jnp.where(allowed, 0.0, MASKED)


def attend_kernel(
    heads, tokens, outer, width,
    place_ref, lin_ref, cos_ref, sin_ref, keydoc_ref, doc_ref,
    mixed_ref, query_ref, key_ref, value_ref, lse_ref,
    key_rows, bias_ref,
):
    length = doc_ref.shape[1]
    key_heads = key_ref.shape[0]
    group = heads // key_heads
    half = HEAD // 2
    place = place_ref[0]
    for block in range(length // tokens):
        source = pl.ds(block_offset(place, block, outer, tokens), tokens)
        lanes = slice(block * tokens, (block + 1) * tokens)
        cosine, sine = cos_ref[:, lanes], sin_ref[:, lanes]
        for head in range(heads + key_heads):
            first = lin_ref[head, 0:half, source]
            second = lin_ref[head, half:HEAD, source]
            one = (first * cosine - second * sine).astype(BF16)
            two = (second * cosine + first * sine).astype(BF16)
            if head < heads:
                scale = jnp.asarray(HEAD ** (-0.5), BF16)
                query_ref[head, 0:half, lanes] = one * scale
                query_ref[head, half:HEAD, lanes] = two * scale
            else:
                key_ref[head - heads, 0:half, lanes] = one
                key_ref[head - heads, half:HEAD, lanes] = two
        for head in range(key_heads):
            value_ref[head, :, lanes] = lin_ref[heads + key_heads + head, :, source].astype(BF16)
    for kv in range(key_heads):
        key_rows[kv] = key_ref[kv].astype(F32).T.astype(BF16)
    for step in range(length // width):
        start = step * width
        reach = start + width
        fill_bias(bias_ref, keydoc_ref, doc_ref, start, width, reach)
        for kv in range(key_heads):

            def one_head(index, carry, kv=kv, start=start, reach=reach):
                head = kv * group + index
                query = query_ref[head, :, start:reach]
                scores = mm(key_rows[kv, 0:reach, :], query, ((1,), (0,))) + bias_ref[0:reach, :]
                top = jnp.max(scores, axis=0, keepdims=True)
                terms = jnp.exp(scores - top)
                total = jnp.sum(terms, axis=0, keepdims=True)
                probs = (terms * (1.0 / total)).astype(BF16)
                mixed = mm(value_ref[kv, :, 0:reach], probs, ((1,), (0,))).astype(BF16)
                for block in range(start // tokens, reach // tokens):
                    target = pl.ds(block_offset(place, block, outer, tokens), tokens)
                    lanes = slice(block * tokens - start, (block + 1) * tokens - start)
                    mixed_ref[head, :, target] = mixed[:, lanes]
                lse_ref[head, :, start:reach] = top + jnp.log(total)
                return carry

            lax.fori_loop(0, group, one_head, 0)


def attend_back_kernel(
    heads, tokens, outer, width,
    place_ref, grad_ref, query_ref, key_ref, value_ref, lse_ref, cos_ref, sin_ref,
    keydoc_ref, doc_ref,
    out_ref,
    key_rows, value_rows, key_grad, value_grad, grad_abs, bias_ref,
):
    length = doc_ref.shape[1]
    key_heads = key_ref.shape[0]
    group = heads // key_heads
    half = HEAD // 2
    scale = HEAD ** (-0.5)
    place = place_ref[0]

    def put_back(head, block, gradient):
        target = pl.ds(block_offset(place, block, outer, tokens), tokens)
        lanes = slice(block * tokens, (block + 1) * tokens)
        cosine, sine = cos_ref[:, lanes], sin_ref[:, lanes]
        one, two = gradient[0:half], gradient[half:HEAD]
        out_ref[head, 0:half, target] = (one * cosine + two * sine).astype(BF16)
        out_ref[head, half:HEAD, target] = (two * cosine - one * sine).astype(BF16)

    for block in range(length // tokens):
        source = pl.ds(block_offset(place, block, outer, tokens), tokens)
        lanes = slice(block * tokens, (block + 1) * tokens)
        for head in range(heads):
            grad_abs[head, :, lanes] = grad_ref[head, :, source]
    for kv in range(key_heads):
        key_rows[kv] = key_ref[kv].astype(F32).T.astype(BF16)
        value_rows[kv] = value_ref[kv].astype(F32).T.astype(BF16)
    key_grad[...] = jnp.zeros_like(key_grad)
    value_grad[...] = jnp.zeros_like(value_grad)
    for step in range(length // width):
        start = step * width
        reach = start + width
        fill_bias(bias_ref, keydoc_ref, doc_ref, start, width, reach)
        for kv in range(key_heads):

            def one_head(index, carry, kv=kv, start=start, reach=reach):
                head = kv * group + index
                query = query_ref[head, :, start:reach]
                grad = grad_abs[head, :, start:reach]
                query_rows = query.astype(F32).T.astype(BF16)
                grad_rows = grad.astype(F32).T.astype(BF16)
                scores = mm(key_rows[kv, 0:reach, :], query, ((1,), (0,))) + bias_ref[0:reach, :]
                probs = jnp.exp(scores - lse_ref[head, :, start:reach])
                grad_probs = mm(value_rows[kv, 0:reach, :], grad, ((1,), (0,)))
                delta = jnp.sum(probs * grad_probs, axis=0, keepdims=True)
                grad_scores = (probs * (grad_probs - delta)).astype(BF16)
                value_grad[kv, 0:reach, :] += mm(probs.astype(BF16), grad_rows, ((1,), (0,)))
                key_grad[kv, 0:reach, :] += mm(grad_scores, query_rows, ((1,), (0,)))
                grad_query = mm(key_ref[kv, :, 0:reach], grad_scores, ((1,), (0,))) * scale
                for block in range(start // tokens, reach // tokens):
                    lanes = slice(block * tokens - start, (block + 1) * tokens - start)
                    put_back(head, block, grad_query[:, lanes])
                return carry

            lax.fori_loop(0, group, one_head, 0)
    for block in range(length // tokens):
        lanes = slice(block * tokens, (block + 1) * tokens)
        target = pl.ds(block_offset(place, block, outer, tokens), tokens)
        for kv in range(key_heads):
            put_back(heads + kv, block, key_grad[kv, lanes, :].T)
            out_ref[heads + key_heads + kv, :, target] = value_grad[kv, lanes, :].T.astype(BF16)


def vmem_spec():
    return pl.BlockSpec(memory_space=pltpu.VMEM)


def attend(place, lin, cosine, sine, keydoc, doc, heads, tokens, outer):
    total, _, length = lin.shape
    key_heads = (total - heads) // 2
    width = min(256, length)
    shape = jax.ShapeDtypeStruct
    return pl.pallas_call(
        functools.partial(attend_kernel, heads, tokens, outer, width),
        out_shape=(
            shape((heads, HEAD, length), BF16),
            shape((heads, HEAD, length), BF16),
            shape((key_heads, HEAD, length), BF16),
            shape((key_heads, HEAD, length), BF16),
            shape((heads, 1, length), F32),
        ),
        in_specs=[pl.BlockSpec(memory_space=pltpu.SMEM)] + [vmem_spec()] * 5,
        out_specs=(vmem_spec(),) * 5,
        scratch_shapes=[
            pltpu.VMEM((key_heads, length, HEAD), BF16),
            pltpu.VMEM((length, width), F32),
        ],
        compiler_params=pltpu.CompilerParams(vmem_limit_bytes=40 * 2**20),
        cost_estimate=pl.CostEstimate(
            flops=heads * length * HEAD,
            bytes_accessed=total * HEAD * length,
            transcendentals=0,
        ),
    )(place, lin, cosine, sine, keydoc, doc)


def attend_back(place, grad, query, key, value, lse, cosine, sine, keydoc, doc, tokens, outer):
    heads, _, length = query.shape
    key_heads = key.shape[0]
    width = min(256, length)
    total = heads + 2 * key_heads
    return pl.pallas_call(
        functools.partial(attend_back_kernel, heads, tokens, outer, width),
        out_shape=jax.ShapeDtypeStruct((total, HEAD, length), BF16),
        in_specs=[pl.BlockSpec(memory_space=pltpu.SMEM)] + [vmem_spec()] * 9,
        out_specs=vmem_spec(),
        scratch_shapes=[
            pltpu.VMEM((key_heads, length, HEAD), BF16),
            pltpu.VMEM((key_heads, length, HEAD), BF16),
            pltpu.VMEM((key_heads, length, HEAD), F32),
            pltpu.VMEM((key_heads, length, HEAD), F32),
            pltpu.VMEM((heads, HEAD, length), BF16),
            pltpu.VMEM((length, width), F32),
        ],
        compiler_params=pltpu.CompilerParams(vmem_limit_bytes=40 * 2**20),
        cost_estimate=pl.CostEstimate(
            flops=heads * length * HEAD,
            bytes_accessed=total * HEAD * length,
            transcendentals=0,
        ),
    )(place, grad, query, key, value, lse, cosine, sine, keydoc, doc)


def join_kernel(down_rows, gate_part, up_part, gate_weight, up_weight, gate_ref, up_ref, sum_ref):
    @pl.when(pl.program_id(0) == 0)
    def _():
        sum_ref[...] = jnp.zeros_like(sum_ref)

    for part, weight, out in ((gate_part, gate_weight, gate_ref), (up_part, up_weight, up_ref)):
        for block in range(part.shape[0]):
            lanes = slice(block * down_rows, (block + 1) * down_rows)
            piece = part[block].astype(F32)
            out[:, lanes] = piece
            term = piece * weight[:, lanes].astype(F32)
            sum_ref[...] += jnp.sum(term, axis=1, keepdims=True)


def join_pair(pair_grad, gate_weight, up_weight, outer, down_rows):
    blocks, rows, _ = pair_grad.shape
    units = gate_weight.shape[1]
    width = blocks * down_rows
    shape = jax.ShapeDtypeStruct
    wide_spec = pl.BlockSpec((rows, width), lambda i: (0, i))
    return pl.pallas_call(
        functools.partial(join_kernel, down_rows),
        grid=(outer,),
        out_shape=(
            shape((rows, units), F32), shape((rows, units), F32), shape((rows, 128), F32),
        ),
        in_specs=[
            pl.BlockSpec((blocks, rows, down_rows), lambda i: (0, 0, i)),
            pl.BlockSpec((blocks, rows, down_rows), lambda i: (0, 0, i + outer)),
            wide_spec,
            wide_spec,
        ],
        out_specs=(wide_spec, wide_spec, pl.BlockSpec((rows, 128), lambda i: (0, 0))),
        compiler_params=pltpu.CompilerParams(vmem_limit_bytes=32 * 2**20),
        cost_estimate=pl.CostEstimate(
            flops=4 * rows * units, bytes_accessed=16 * rows * units, transcendentals=0
        ),
    )(pair_grad, pair_grad, gate_weight, up_weight)


def exchange(value, axis, size, step):
    return lax.ppermute(value, axis, [(i, i ^ step) for i in range(size)])


def put(buffer, piece, index):
    return lax.dynamic_update_slice(
        buffer, piece, tuple(jnp.asarray(i, jnp.int32) for i in index)
    )


def pick(value, index, axis=0):
    return lax.dynamic_index_in_dim(value, index, axis, keepdims=False)


def after(value, *marks):
    return lax.optimization_barrier((value,) + marks)[0]


def make_program(wide, narrow):
    outer = wide // INNER
    near_size = INNER * narrow
    near_groups = [[o * near_size + i for i in range(near_size)] for o in range(outer)]
    chip_groups = [[c + INNER * o for o in range(outer)] for c in range(INNER)]
    both = ("wide", "narrow")

    def core_swap(value):
        return exchange(value, "wide", wide, 1)

    def outer_swap(value, step):
        return exchange(value, "wide", wide, INNER * step)

    def narrow_swap(value, step):
        return exchange(value, "narrow", narrow, step)

    def fan_out(value, swap, size):
        return [value] + [swap(value, step) for step in range(1, size)]

    def narrow_gather(value):
        spread = jnp.broadcast_to(value[None], (narrow,) + value.shape)
        return lax.all_to_all(spread, "narrow", 0, 0, tiled=True)

    def narrow_sum(total):
        split = total.reshape(narrow, -1, total.shape[-1])
        return lax.all_to_all(split, "narrow", 0, 0, tiled=True)

    def with_sibling(first):
        return jnp.concatenate([first, core_swap(first)], axis=0)

    def join_near(parts):
        first = jnp.concatenate(parts, axis=0)
        return jnp.concatenate([first, core_swap(first)], axis=0)

    def near_total(product):
        arrived = core_swap(product(1).astype(BF16))
        return (product(0) + arrived.astype(F32)).astype(BF16), arrived

    def scatter(total, swap, size):
        split = total.reshape(size, -1, total.shape[-1])
        return [split[0]] + [swap(split[step], step) for step in range(1, size)]

    def add_up(parts):
        total = parts[0].astype(F32)
        for piece in parts[1:]:
            total = total + piece.astype(F32)
        return total

    def per_device(
        layer_input, output_grad, doc_ids, keep_mask, attention_gain, query_weight, key_weight,
        value_weight, out_weight, feedforward_gain, gate_weight, up_weight, down_weight,
    ):
        tokens = layer_input.shape[1]
        model = layer_input.shape[2]
        rows = query_weight.shape[0]
        down_rows = down_weight.shape[0]
        kv_total = key_weight.shape[1] // HEAD
        heads = HEADS // wide
        group = HEADS // kv_total
        key_heads = max(1, heads // group)
        repeat = max(1, group // heads)
        place = lax.axis_index("wide")
        chip = place // INNER
        layer = lax.axis_index("narrow")
        core = place % INNER
        place_arg = place.reshape(1).astype(jnp.int32)

        head_cols = heads * HEAD
        kv_cols = key_heads * HEAD

        def kv_split(weight):
            parts = weight.reshape(rows, -1, kv_cols)
            return jnp.repeat(parts, repeat, axis=1)

        packed = jnp.concatenate(
            [query_weight.reshape(rows, wide, head_cols), kv_split(key_weight), kv_split(value_weight)],
            axis=2,
        )
        cols = packed.shape[2]
        own_input = layer_input[0]
        residual = own_input.astype(F32)
        out_parts = fan_out(out_weight, narrow_swap, narrow)
        packed = packed.transpose(1, 0, 2)
        gain_rows = -(-2 * rows // cols) * 8
        gains = jnp.concatenate([attention_gain, feedforward_gain])
        gains = jnp.pad(gains, (0, gain_rows * cols - 2 * rows)).reshape(1, gain_rows, cols)
        gains = jnp.broadcast_to(gains, (wide, gain_rows, cols))
        packed = jnp.concatenate([packed, gains], axis=1)
        by_wide = lax.all_to_all(packed, "wide", 0, 0, tiled=True)
        input_parts = fan_out(after(own_input, by_wide), outer_swap, outer)

        weight_parts = fan_out(after(by_wide, *out_parts), narrow_swap, narrow)

        def for_group(weight):
            return weight.reshape(rows, outer, near_size, down_rows).transpose(2, 0, 1, 3)

        pair_cols = 2 * outer * down_rows
        units = pair_cols // 2
        pair_weight = jnp.stack([for_group(gate_weight), for_group(up_weight)], axis=2)
        pair_weight = pair_weight.reshape(near_size, rows, pair_cols)
        pair_weight = after(pair_weight, *weight_parts, *input_parts)
        column = lax.all_to_all(
            pair_weight, both, 0, 0, axis_index_groups=near_groups, tiled=True
        )
        down = lax.all_gather(
            down_weight, "wide", axis=0, tiled=True, axis_index_groups=chip_groups
        )

        all_input = join_near(input_parts)
        scaled_all, factor_all = normalize(all_input.astype(F32))
        attention_weight = after(jnp.zeros((wide, narrow, rows, cols), BF16), factor_all)
        for step, piece in enumerate(weight_parts):
            attention_weight = put(
                attention_weight, piece[:, None, :rows], (0, layer ^ step, 0, 0)
            )
        attention_weight = attention_weight.reshape(model, cols)
        lines = jnp.stack([piece[:, rows, : 2 * rows] for piece in weight_parts], axis=1)
        lines = jnp.stack([pick(lines, layer ^ step, 1) for step in range(narrow)], axis=1)
        lines = lines.astype(F32)
        gain_one = lines[:, :, :rows].reshape(1, model)
        gain_two = lines[:, :, rows:].reshape(1, model)

        out_own = jnp.zeros((narrow, rows, model), BF16)
        for step, piece in enumerate(out_parts):
            out_own = put(out_own, piece[None], (layer ^ step, 0, 0))
        out_own = out_own.reshape(narrow * rows, model)

        grad_out_own = output_grad[0]
        grad_out_near = narrow_gather(after(grad_out_own, column)).reshape(-1, model)

        own = all_input.shape[0] // INNER
        documents = doc_ids[0]
        positions = stream_positions(documents)
        angles = jnp.asarray(inverse_rates(HEAD))[:, None] * positions.astype(F32)[None, :]
        cosine, sine = jnp.cos(angles), jnp.sin(angles)
        keydoc = jnp.where(keep_mask[0] > 0, documents, -1)[:, None]
        doc = documents[None, :]
        normed_one = (scaled_all * gain_one).astype(BF16)
        lin = mm(attention_weight, normed_one, ((0,), (1,)))
        lin = lin.reshape(-1, HEAD, lin.shape[1])
        mixed, query, key, value, lse = attend(
            place_arg, lin, cosine, sine, keydoc, doc, heads, tokens, outer
        )
        mixed = mixed.reshape(head_cols, -1)

        def out_product(near):
            return mm(mixed[:, near * own : (near + 1) * own], out_own, ((0,), (0,)))

        attended, _ = near_total(out_product)
        gate_up = lax.all_gather(
            after(column.reshape(near_size * rows, pair_cols), down, attended), "wide",
            axis=0, tiled=True, axis_index_groups=chip_groups,
        )
        piece = tokens // HALVES
        attended = attended.reshape(outer, HALVES, piece, model)
        residual_half = residual.reshape(HALVES, piece, model)
        after_half, scaled_half, factor_half, normed_half = [], [], [], []
        attended_parts = [
            [attended[0, h]] + [outer_swap(attended[step, h], step) for step in range(1, outer)]
            for h in range(HALVES)
        ]
        attended_parts[0][0] = after(attended_parts[0][0], grad_out_near)
        for h in range(HALVES):
            after_half.append(residual_half[h] + add_up(attended_parts[h]))
            scaled, factor = normalize(after_half[h])
            scaled_half.append(scaled)
            factor_half.append(factor)
            normed_half.append((scaled * gain_two).astype(BF16))

        half = narrow * piece
        first = grad_out_near.reshape(narrow, HALVES, piece, model).transpose(1, 0, 2, 3)
        grad_out = jnp.stack([first, core_swap(first)], axis=1).reshape(HALVES, -1, model)
        normed_two, hidden, grad_pair, two_totals, two_parts, branch_totals = [], [], [], [], [], []
        near_half = [narrow_gather(normed_half[h]).reshape(-1, model) for h in range(HALVES)]
        for h in range(HALVES):
            normed_near = after(near_half[h], two_totals[h - 1]) if h else near_half[h]
            normed_two.append(with_sibling(normed_near))
            pair = mm(normed_two[h], gate_up, ((1,), (0,)))
            gate, upward = pair[:, :units], pair[:, units:]
            sigmoid_gate = jax.nn.sigmoid(gate)
            activated = gate * sigmoid_gate
            hidden.append((activated * upward).astype(BF16))
            grad_hidden = mm(grad_out[h], down, ((1,), (1,)))
            slope = sigmoid_gate * (1.0 + gate * (1.0 - sigmoid_gate))
            grad_gate = (grad_hidden * upward * slope).astype(BF16)
            grad_up = (grad_hidden * activated).astype(BF16)
            both_grads = jnp.concatenate([grad_gate, grad_up], axis=1)
            grad_pair.append(both_grads)
            if not h:
                both_grads = after(both_grads, near_half[-1])

            def two_product(near, both_grads=both_grads):
                return mm(both_grads[near * half : (near + 1) * half], gate_up, ((1,), (1,)))

            two_totals.append(near_total(two_product)[0])
            total = two_totals[h] if not h else after(two_totals[h], two_parts[h - 1])
            two_parts.append(
                lax.psum_scatter(total, "narrow", scatter_dimension=0, tiled=True)
            )

        for h in range(HALVES):
            late_hidden = after(hidden[h], two_totals[-1], two_parts[0])

            def branch_product(near, late_hidden=late_hidden):
                return mm(late_hidden[near * half : (near + 1) * half], down, ((1,), (0,)))

            branch_totals.append(near_total(branch_product)[0])

        pair_term = mm(
            jnp.concatenate(normed_two, axis=0), jnp.concatenate(grad_pair, axis=0), ((0,), (0,))
        ).astype(BF16)
        pair_sum = lax.psum_scatter(
            after(pair_term, two_parts[-1], branch_totals[-1]), "wide", scatter_dimension=0, tiled=True,
            axis_index_groups=chip_groups,
        )

        grad_two = jnp.concatenate(two_parts, axis=0).astype(F32)
        scaled_two = jnp.concatenate(scaled_half, axis=0)
        factor_two = jnp.concatenate(factor_half, axis=0)
        grad_scaled_two = grad_two * gain_two
        grad_middle = grad_out_own.astype(F32) + factor_two * (
            grad_scaled_two
            - scaled_two * jnp.mean(grad_scaled_two * scaled_two, axis=-1, keepdims=True)
        )
        middle_parts = fan_out(grad_middle.astype(BF16), outer_swap, outer)
        branch_total = jnp.stack(
            [total.reshape(narrow, piece, model) for total in branch_totals], axis=1
        ).reshape(-1, model)
        branch_parts = narrow_sum(after(branch_total, middle_parts[0]))
        after_attention = jnp.concatenate(after_half, axis=0)
        layer_output = after_attention + jnp.sum(branch_parts.astype(F32), axis=0)
        down_term = mm(
            jnp.concatenate([after(hidden[0], middle_parts[0])] + hidden[1:], axis=0),
            grad_out.reshape(-1, model), ((0,), (0,)),
        ).astype(BF16)
        middle_parts[0] = after(middle_parts[0], down_term)
        near_middle = lax.optimization_barrier(jnp.concatenate(middle_parts, axis=0))
        grad_attention = after(with_sibling(near_middle), branch_parts)
        out_term = mm(mixed, grad_attention, ((1,), (0,))).astype(BF16)
        out_term = out_term.reshape(narrow, rows, model)
        out_split = [pick(out_term, layer ^ step) for step in range(narrow)]
        out_sent = [narrow_swap(out_split[step], step) for step in range(1, narrow)]
        grad_mixed = mm(out_own, after(grad_attention, *out_split), ((1,), (1,)))
        grad_mixed = grad_mixed.astype(BF16)
        grad_lin = attend_back(
            place_arg, grad_mixed.reshape(heads, HEAD, -1), query, key, value, lse, cosine, sine,
            keydoc, doc, tokens, outer,
        ).reshape(cols, -1)
        grad_lin = after(grad_lin, *out_sent)

        def one_product(near):
            return mm(grad_lin[:, near * own : (near + 1) * own], attention_weight, ((0,), (1,)))

        one_total, one_swapped = near_total(one_product)
        one_parts = scatter(one_total, outer_swap, outer)
        grad_one = add_up(one_parts)
        scaled_one, factor_one = normalize(residual)
        grad_scaled_one = grad_one * gain_one
        input_grad = grad_middle + factor_one * (
            grad_scaled_one
            - scaled_one * jnp.mean(grad_scaled_one * scaled_one, axis=-1, keepdims=True)
        )

        late_lin = after(grad_lin, one_swapped)
        lin_term = mm(normed_one, late_lin, ((0,), (1,))).astype(BF16)
        lin_term = lin_term.reshape(wide, narrow, rows, cols).transpose(1, 0, 2, 3)
        out_grad = add_up([after(out_split[0], lin_term)] + out_sent)
        lin_sum = jnp.sum(lax.all_to_all(lin_term, "narrow", 0, 0, tiled=True).astype(F32), axis=0)
        lin_split = lin_sum.astype(BF16).reshape(outer, INNER, rows, cols)
        mine = pick(lin_split, core, 1)
        other = core_swap(pick(lin_split, 1 - core, 1))
        lin_pair = jnp.stack([mine, other], axis=1)
        lin_parts = [pick(lin_pair, chip)] + [
            outer_swap(pick(lin_pair, chip ^ step), step) for step in range(1, outer)
        ]
        lin_parts = jnp.concatenate(lin_parts, axis=0)
        lin_grad = jnp.stack([pick(lin_parts, place ^ w) for w in range(wide)]).astype(F32)
        down_grad = lax.psum_scatter(
            after(down_term, pair_sum, lin_term), "wide", scatter_dimension=0, tiled=True,
            axis_index_groups=chip_groups,
        ).astype(F32)

        pair_sum = after(pair_sum, lin_sum, one_parts[0]).reshape(near_size, rows, pair_cols)
        pair_grad = lax.all_to_all(pair_sum, both, 0, 0, axis_index_groups=near_groups, tiled=True)
        if down_rows % 128 == 0:
            gate_grad, up_grad, gain_sum = join_pair(
                pair_grad, gate_weight, up_weight, outer, down_rows
            )
            gain_sum = gain_sum[:, 0]
        else:
            pair_grad = pair_grad.reshape(near_size, rows, 2, outer, down_rows)
            pair_grad = pair_grad.transpose(2, 1, 3, 0, 4).reshape(2, rows, -1).astype(F32)
            gate_grad, up_grad = pair_grad[0], pair_grad[1]
            gain_sum = jnp.sum(gate_grad * gate_weight.astype(F32), axis=1) + jnp.sum(
                up_grad * up_weight.astype(F32), axis=1
            )
        gain_two_grad = gain_sum / feedforward_gain.astype(F32)

        query_grad = lin_grad[:, :, :head_cols].transpose(1, 0, 2).reshape(rows, -1)

        def kv_join(part):
            joined = part.reshape(wide // repeat, repeat, rows, kv_cols).sum(axis=1)
            return joined.transpose(1, 0, 2).reshape(rows, -1)

        key_grad = kv_join(lin_grad[:, :, head_cols : head_cols + kv_cols])
        value_grad = kv_join(lin_grad[:, :, head_cols + kv_cols :])
        gain_one_grad = (
            jnp.sum(query_grad * query_weight.astype(F32), axis=1)
            + jnp.sum(key_grad * key_weight.astype(F32), axis=1)
            + jnp.sum(value_grad * value_weight.astype(F32), axis=1)
        ) / attention_gain.astype(F32)
        return (
            layer_output[None].astype(BF16),
            input_grad[None].astype(BF16),
            gain_one_grad,
            query_grad,
            key_grad,
            value_grad,
            out_grad,
            gain_two_grad,
            gate_grad,
            up_grad,
            down_grad,
        )

    return per_device


def solution(mesh):
    rows = P(("wide", "narrow"), None)
    line = P(("wide", "narrow"))
    stream = P("narrow", "wide", None)
    return jax.shard_map(
        make_program(mesh.shape["wide"], mesh.shape["narrow"]),
        mesh=mesh,
        in_specs=(
            stream, stream, P("narrow", None), P("narrow", None),
            line, rows, rows, rows, rows, line, rows, rows, rows,
        ),
        out_specs=(stream, stream, line, rows, rows, rows, rows, line, rows, rows, rows),
        check_vma=False,
    )
```

```python
import functools

import jax
import jax.numpy as jnp
import numpy as np
from jax import lax
from jax.experimental import pallas as pl
from jax.experimental.pallas import tpu as pltpu
from jax.sharding import PartitionSpec as P

HEADS = 32
HEAD = 64
DOCS = 3
EPSILON = 1e-05
MASKED = -1e30
INNER = 2
HALVES = 2
F32 = jnp.float32
BF16 = jnp.bfloat16


def inverse_rates(head_width):
    plain = 500000.0 ** (-(np.arange(0, head_width, 2) * 1.0) / head_width)
    wavelength = 2.0 * np.pi / plain
    smooth = (8192.0 / wavelength - 1.0) / 3.0
    blended = (1.0 - smooth) * plain / 32.0 + smooth * plain
    scaled = np.where(
        wavelength > 8192.0, plain / 32.0, np.where(wavelength < 2048.0, plain, blended)
    )
    return scaled.astype(np.float32)


def stream_positions(documents):
    numbers = jnp.arange(DOCS, dtype=jnp.int32)
    starts = jnp.sum((documents[None, :] < numbers[:, None]).astype(jnp.int32), axis=1)
    own_start = jnp.sum(
        jnp.where(documents[:, None] == numbers[None, :], starts[None, :], 0), axis=1
    )
    return jnp.arange(documents.shape[0], dtype=jnp.int32) - own_start


def normalize(values):
    factor = lax.rsqrt(jnp.mean(values * values, axis=-1, keepdims=True) + EPSILON)
    return values * factor, factor


def mm(left, right, dims):
    return lax.dot_general(left, right, (dims, ((), ())), preferred_element_type=F32)


def block_offset(place, block, outer, tokens):
    peer = place ^ block
    return pl.multiple_of(((peer % INNER) * outer + peer // INNER) * tokens, tokens)


def fill_bias(bias_ref, keydoc_ref, doc_ref, start, width, length):
    shape = (length, width)
    key_index = lax.broadcasted_iota(jnp.int32, shape, 0)
    query_index = lax.broadcasted_iota(jnp.int32, shape, 1) + start
    allowed = (keydoc_ref[0:length, :] == doc_ref[:, start : start + width]) & (
        key_index <= query_index
    )
    bias_ref[0:length, :] = jnp.where(allowed, 0.0, MASKED)


def attend_kernel(
    heads, tokens, outer, width,
    place_ref, lin_ref, cos_ref, sin_ref, keydoc_ref, doc_ref,
    mixed_ref, query_ref, key_ref, value_ref, lse_ref,
    key_rows, bias_ref,
):
    length = doc_ref.shape[1]
    key_heads = key_ref.shape[0]
    group = heads // key_heads
    half = HEAD // 2
    place = place_ref[0]
    for block in range(length // tokens):
        source = pl.ds(block_offset(place, block, outer, tokens), tokens)
        lanes = slice(block * tokens, (block + 1) * tokens)
        cosine, sine = cos_ref[:, lanes], sin_ref[:, lanes]
        for head in range(heads + key_heads):
            first = lin_ref[head, 0:half, source]
            second = lin_ref[head, half:HEAD, source]
            one = (first * cosine - second * sine).astype(BF16)
            two = (second * cosine + first * sine).astype(BF16)
            if head < heads:
                scale = jnp.asarray(HEAD ** (-0.5), BF16)
                query_ref[head, 0:half, lanes] = one * scale
                query_ref[head, half:HEAD, lanes] = two * scale
            else:
                key_ref[head - heads, 0:half, lanes] = one
                key_ref[head - heads, half:HEAD, lanes] = two
        for head in range(key_heads):
            value_ref[head, :, lanes] = lin_ref[heads + key_heads + head, :, source].astype(BF16)
    for kv in range(key_heads):
        key_rows[kv] = key_ref[kv].astype(F32).T.astype(BF16)
    for step in range(length // width):
        start = step * width
        reach = start + width
        fill_bias(bias_ref, keydoc_ref, doc_ref, start, width, reach)
        for kv in range(key_heads):

            def one_head(index, carry, kv=kv, start=start, reach=reach):
                head = kv * group + index
                query = query_ref[head, :, start:reach]
                scores = mm(key_rows[kv, 0:reach, :], query, ((1,), (0,))) + bias_ref[0:reach, :]
                top = jnp.max(scores, axis=0, keepdims=True)
                terms = jnp.exp(scores - top)
                total = jnp.sum(terms, axis=0, keepdims=True)
                probs = (terms * (1.0 / total)).astype(BF16)
                mixed = mm(value_ref[kv, :, 0:reach], probs, ((1,), (0,))).astype(BF16)
                for block in range(start // tokens, reach // tokens):
                    target = pl.ds(block_offset(place, block, outer, tokens), tokens)
                    lanes = slice(block * tokens - start, (block + 1) * tokens - start)
                    mixed_ref[head, :, target] = mixed[:, lanes]
                lse_ref[head, :, start:reach] = top + jnp.log(total)
                return carry

            lax.fori_loop(0, group, one_head, 0)


def attend_back_kernel(
    heads, tokens, outer, width,
    place_ref, grad_ref, query_ref, key_ref, value_ref, lse_ref, cos_ref, sin_ref,
    keydoc_ref, doc_ref,
    out_ref,
    key_rows, value_rows, key_grad, value_grad, grad_abs, bias_ref,
):
    length = doc_ref.shape[1]
    key_heads = key_ref.shape[0]
    group = heads // key_heads
    half = HEAD // 2
    scale = HEAD ** (-0.5)
    place = place_ref[0]

    def put_back(head, block, gradient):
        target = pl.ds(block_offset(place, block, outer, tokens), tokens)
        lanes = slice(block * tokens, (block + 1) * tokens)
        cosine, sine = cos_ref[:, lanes], sin_ref[:, lanes]
        one, two = gradient[0:half], gradient[half:HEAD]
        out_ref[head, 0:half, target] = (one * cosine + two * sine).astype(BF16)
        out_ref[head, half:HEAD, target] = (two * cosine - one * sine).astype(BF16)

    for block in range(length // tokens):
        source = pl.ds(block_offset(place, block, outer, tokens), tokens)
        lanes = slice(block * tokens, (block + 1) * tokens)
        for head in range(heads):
            grad_abs[head, :, lanes] = grad_ref[head, :, source]
    for kv in range(key_heads):
        key_rows[kv] = key_ref[kv].astype(F32).T.astype(BF16)
        value_rows[kv] = value_ref[kv].astype(F32).T.astype(BF16)
    key_grad[...] = jnp.zeros_like(key_grad)
    value_grad[...] = jnp.zeros_like(value_grad)
    for step in range(length // width):
        start = step * width
        reach = start + width
        fill_bias(bias_ref, keydoc_ref, doc_ref, start, width, reach)
        for kv in range(key_heads):

            def one_head(index, carry, kv=kv, start=start, reach=reach):
                head = kv * group + index
                query = query_ref[head, :, start:reach]
                grad = grad_abs[head, :, start:reach]
                query_rows = query.astype(F32).T.astype(BF16)
                grad_rows = grad.astype(F32).T.astype(BF16)
                scores = mm(key_rows[kv, 0:reach, :], query, ((1,), (0,))) + bias_ref[0:reach, :]
                probs = jnp.exp(scores - lse_ref[head, :, start:reach])
                grad_probs = mm(value_rows[kv, 0:reach, :], grad, ((1,), (0,)))
                delta = jnp.sum(probs * grad_probs, axis=0, keepdims=True)
                grad_scores = (probs * (grad_probs - delta)).astype(BF16)
                value_grad[kv, 0:reach, :] += mm(probs.astype(BF16), grad_rows, ((1,), (0,)))
                key_grad[kv, 0:reach, :] += mm(grad_scores, query_rows, ((1,), (0,)))
                grad_query = mm(key_ref[kv, :, 0:reach], grad_scores, ((1,), (0,))) * scale
                for block in range(start // tokens, reach // tokens):
                    lanes = slice(block * tokens - start, (block + 1) * tokens - start)
                    put_back(head, block, grad_query[:, lanes])
                return carry

            lax.fori_loop(0, group, one_head, 0)
    for block in range(length // tokens):
        lanes = slice(block * tokens, (block + 1) * tokens)
        target = pl.ds(block_offset(place, block, outer, tokens), tokens)
        for kv in range(key_heads):
            put_back(heads + kv, block, key_grad[kv, lanes, :].T)
            out_ref[heads + key_heads + kv, :, target] = value_grad[kv, lanes, :].T.astype(BF16)


def vmem_spec():
    return pl.BlockSpec(memory_space=pltpu.VMEM)


def attend(place, lin, cosine, sine, keydoc, doc, heads, tokens, outer):
    total, _, length = lin.shape
    key_heads = (total - heads) // 2
    width = min(256, length)
    shape = jax.ShapeDtypeStruct
    return pl.pallas_call(
        functools.partial(attend_kernel, heads, tokens, outer, width),
        out_shape=(
            shape((heads, HEAD, length), BF16),
            shape((heads, HEAD, length), BF16),
            shape((key_heads, HEAD, length), BF16),
            shape((key_heads, HEAD, length), BF16),
            shape((heads, 1, length), F32),
        ),
        in_specs=[pl.BlockSpec(memory_space=pltpu.SMEM)] + [vmem_spec()] * 5,
        out_specs=(vmem_spec(),) * 5,
        scratch_shapes=[
            pltpu.VMEM((key_heads, length, HEAD), BF16),
            pltpu.VMEM((length, width), F32),
        ],
        compiler_params=pltpu.CompilerParams(vmem_limit_bytes=40 * 2**20),
        cost_estimate=pl.CostEstimate(
            flops=heads * length * HEAD,
            bytes_accessed=total * HEAD * length,
            transcendentals=0,
        ),
    )(place, lin, cosine, sine, keydoc, doc)


def attend_back(place, grad, query, key, value, lse, cosine, sine, keydoc, doc, tokens, outer):
    heads, _, length = query.shape
    key_heads = key.shape[0]
    width = min(256, length)
    total = heads + 2 * key_heads
    return pl.pallas_call(
        functools.partial(attend_back_kernel, heads, tokens, outer, width),
        out_shape=jax.ShapeDtypeStruct((total, HEAD, length), BF16),
        in_specs=[pl.BlockSpec(memory_space=pltpu.SMEM)] + [vmem_spec()] * 9,
        out_specs=vmem_spec(),
        scratch_shapes=[
            pltpu.VMEM((key_heads, length, HEAD), BF16),
            pltpu.VMEM((key_heads, length, HEAD), BF16),
            pltpu.VMEM((key_heads, length, HEAD), F32),
            pltpu.VMEM((key_heads, length, HEAD), F32),
            pltpu.VMEM((heads, HEAD, length), BF16),
            pltpu.VMEM((length, width), F32),
        ],
        compiler_params=pltpu.CompilerParams(vmem_limit_bytes=40 * 2**20),
        cost_estimate=pl.CostEstimate(
            flops=heads * length * HEAD,
            bytes_accessed=total * HEAD * length,
            transcendentals=0,
        ),
    )(place, grad, query, key, value, lse, cosine, sine, keydoc, doc)


def join_kernel(down_rows, gate_part, up_part, gate_weight, up_weight, gate_ref, up_ref, sum_ref):
    @pl.when(pl.program_id(0) == 0)
    def _():
        sum_ref[...] = jnp.zeros_like(sum_ref)

    for part, weight, out in ((gate_part, gate_weight, gate_ref), (up_part, up_weight, up_ref)):
        for block in range(part.shape[0]):
            lanes = slice(block * down_rows, (block + 1) * down_rows)
            piece = part[block].astype(F32)
            out[:, lanes] = piece
            term = piece * weight[:, lanes].astype(F32)
            sum_ref[...] += jnp.sum(term, axis=1, keepdims=True)


def join_pair(pair_grad, gate_weight, up_weight, outer, down_rows):
    blocks, rows, _ = pair_grad.shape
    units = gate_weight.shape[1]
    width = blocks * down_rows
    shape = jax.ShapeDtypeStruct
    wide_spec = pl.BlockSpec((rows, width), lambda i: (0, i))
    return pl.pallas_call(
        functools.partial(join_kernel, down_rows),
        grid=(outer,),
        out_shape=(
            shape((rows, units), F32), shape((rows, units), F32), shape((rows, 128), F32),
        ),
        in_specs=[
            pl.BlockSpec((blocks, rows, down_rows), lambda i: (0, 0, i)),
            pl.BlockSpec((blocks, rows, down_rows), lambda i: (0, 0, i + outer)),
            wide_spec,
            wide_spec,
        ],
        out_specs=(wide_spec, wide_spec, pl.BlockSpec((rows, 128), lambda i: (0, 0))),
        compiler_params=pltpu.CompilerParams(vmem_limit_bytes=32 * 2**20),
        cost_estimate=pl.CostEstimate(
            flops=4 * rows * units, bytes_accessed=16 * rows * units, transcendentals=0
        ),
    )(pair_grad, pair_grad, gate_weight, up_weight)


def exchange(value, axis, size, step):
    return lax.ppermute(value, axis, [(i, i ^ step) for i in range(size)])


def put(buffer, piece, index):
    return lax.dynamic_update_slice(
        buffer, piece, tuple(jnp.asarray(i, jnp.int32) for i in index)
    )


def pick(value, index, axis=0):
    return lax.dynamic_index_in_dim(value, index, axis, keepdims=False)


def after(value, *marks):
    return lax.optimization_barrier((value,) + marks)[0]


def make_program(wide, narrow):
    outer = wide // INNER
    near_size = INNER * narrow
    near_groups = [[o * near_size + i for i in range(near_size)] for o in range(outer)]
    chip_groups = [[c + INNER * o for o in range(outer)] for c in range(INNER)]
    both = ("wide", "narrow")

    def core_swap(value):
        return exchange(value, "wide", wide, 1)

    def outer_swap(value, step):
        return exchange(value, "wide", wide, INNER * step)

    def narrow_swap(value, step):
        return exchange(value, "narrow", narrow, step)

    def fan_out(value, swap, size):
        return [value] + [swap(value, step) for step in range(1, size)]

    def narrow_gather(value):
        spread = jnp.broadcast_to(value[None], (narrow,) + value.shape)
        return lax.all_to_all(spread, "narrow", 0, 0, tiled=True)

    def narrow_sum(total):
        split = total.reshape(narrow, -1, total.shape[-1])
        return lax.all_to_all(split, "narrow", 0, 0, tiled=True)

    def with_sibling(first):
        return jnp.concatenate([first, core_swap(first)], axis=0)

    def join_near(parts):
        first = jnp.concatenate(parts, axis=0)
        return jnp.concatenate([first, core_swap(first)], axis=0)

    def near_total(product):
        arrived = core_swap(product(1).astype(BF16))
        return (product(0) + arrived.astype(F32)).astype(BF16), arrived

    def scatter(total, swap, size):
        split = total.reshape(size, -1, total.shape[-1])
        return [split[0]] + [swap(split[step], step) for step in range(1, size)]

    def add_up(parts):
        total = parts[0].astype(F32)
        for piece in parts[1:]:
            total = total + piece.astype(F32)
        return total

    def per_device(
        layer_input, output_grad, doc_ids, keep_mask, attention_gain, query_weight, key_weight,
        value_weight, out_weight, feedforward_gain, gate_weight, up_weight, down_weight,
    ):
        tokens = layer_input.shape[1]
        model = layer_input.shape[2]
        rows = query_weight.shape[0]
        down_rows = down_weight.shape[0]
        kv_total = key_weight.shape[1] // HEAD
        heads = HEADS // wide
        group = HEADS // kv_total
        key_heads = max(1, heads // group)
        repeat = max(1, group // heads)
        place = lax.axis_index("wide")
        chip = place // INNER
        layer = lax.axis_index("narrow")
        core = place % INNER
        place_arg = place.reshape(1).astype(jnp.int32)

        head_cols = heads * HEAD
        kv_cols = key_heads * HEAD

        def kv_split(weight):
            parts = weight.reshape(rows, -1, kv_cols)
            return jnp.repeat(parts, repeat, axis=1)

        packed = jnp.concatenate(
            [query_weight.reshape(rows, wide, head_cols), kv_split(key_weight), kv_split(value_weight)],
            axis=2,
        )
        cols = packed.shape[2]
        own_input = layer_input[0]
        residual = own_input.astype(F32)
        out_parts = fan_out(out_weight, narrow_swap, narrow)
        packed = packed.transpose(1, 0, 2)
        gain_rows = -(-2 * rows // cols) * 8
        gains = jnp.concatenate([attention_gain, feedforward_gain])
        gains = jnp.pad(gains, (0, gain_rows * cols - 2 * rows)).reshape(1, gain_rows, cols)
        gains = jnp.broadcast_to(gains, (wide, gain_rows, cols))
        packed = jnp.concatenate([packed, gains], axis=1)
        by_wide = lax.all_to_all(packed, "wide", 0, 0, tiled=True)
        input_parts = fan_out(after(own_input, by_wide), outer_swap, outer)

        weight_parts = fan_out(after(by_wide, *out_parts), narrow_swap, narrow)

        def for_group(weight):
            return weight.reshape(rows, outer, near_size, down_rows).transpose(2, 0, 1, 3)

        pair_cols = 2 * outer * down_rows
        units = pair_cols // 2
        pair_weight = jnp.stack([for_group(gate_weight), for_group(up_weight)], axis=2)
        pair_weight = pair_weight.reshape(near_size, rows, pair_cols)
        pair_weight = after(pair_weight, *weight_parts, *input_parts)
        column = lax.all_to_all(
            pair_weight, both, 0, 0, axis_index_groups=near_groups, tiled=True
        )
        down = lax.all_gather(
            down_weight, "wide", axis=0, tiled=True, axis_index_groups=chip_groups
        )

        all_input = join_near(input_parts)
        scaled_all, factor_all = normalize(all_input.astype(F32))
        attention_weight = after(jnp.zeros((wide, narrow, rows, cols), BF16), factor_all)
        for step, piece in enumerate(weight_parts):
            attention_weight = put(
                attention_weight, piece[:, None, :rows], (0, layer ^ step, 0, 0)
            )
        attention_weight = attention_weight.reshape(model, cols)
        lines = jnp.stack([piece[:, rows, : 2 * rows] for piece in weight_parts], axis=1)
        lines = jnp.stack([pick(lines, layer ^ step, 1) for step in range(narrow)], axis=1)
        lines = lines.astype(F32)
        gain_one = lines[:, :, :rows].reshape(1, model)
        gain_two = lines[:, :, rows:].reshape(1, model)

        out_own = jnp.zeros((narrow, rows, model), BF16)
        for step, piece in enumerate(out_parts):
            out_own = put(out_own, piece[None], (layer ^ step, 0, 0))
        out_own = out_own.reshape(narrow * rows, model)

        grad_out_own = output_grad[0]
        grad_out_near = narrow_gather(after(grad_out_own, column)).reshape(-1, model)

        own = all_input.shape[0] // INNER
        documents = doc_ids[0]
        positions = stream_positions(documents)
        angles = jnp.asarray(inverse_rates(HEAD))[:, None] * positions.astype(F32)[None, :]
        cosine, sine = jnp.cos(angles), jnp.sin(angles)
        keydoc = jnp.where(keep_mask[0] > 0, documents, -1)[:, None]
        doc = documents[None, :]
        normed_one = (scaled_all * gain_one).astype(BF16)
        lin = mm(attention_weight, normed_one, ((0,), (1,)))
        lin = lin.reshape(-1, HEAD, lin.shape[1])
        mixed, query, key, value, lse = attend(
            place_arg, lin, cosine, sine, keydoc, doc, heads, tokens, outer
        )
        mixed = mixed.reshape(head_cols, -1)

        def out_product(near):
            return mm(mixed[:, near * own : (near + 1) * own], out_own, ((0,), (0,)))

        attended, _ = near_total(out_product)
        gate_up = lax.all_gather(
            after(column.reshape(near_size * rows, pair_cols), down, attended), "wide",
            axis=0, tiled=True, axis_index_groups=chip_groups,
        )
        piece = tokens // HALVES
        attended = attended.reshape(outer, HALVES, piece, model)
        residual_half = residual.reshape(HALVES, piece, model)
        after_half, scaled_half, factor_half, normed_half = [], [], [], []
        attended_parts = [
            [attended[0, h]] + [outer_swap(attended[step, h], step) for step in range(1, outer)]
            for h in range(HALVES)
        ]
        attended_parts[0][0] = after(attended_parts[0][0], grad_out_near)
        for h in range(HALVES):
            after_half.append(residual_half[h] + add_up(attended_parts[h]))
            scaled, factor = normalize(after_half[h])
            scaled_half.append(scaled)
            factor_half.append(factor)
            normed_half.append((scaled * gain_two).astype(BF16))

        half = narrow * piece
        first = grad_out_near.reshape(narrow, HALVES, piece, model).transpose(1, 0, 2, 3)
        first_far = core_swap(first)
        grad_out = jnp.stack([first, first_far], axis=1).reshape(HALVES, -1, model)
        normed_two, hidden, grad_pair, two_totals, two_parts, branch_totals = [], [], [], [], [], []
        near_half = [narrow_gather(normed_half[h]).reshape(-1, model) for h in range(HALVES)]
        for h in range(HALVES):
            normed_near = after(near_half[h], two_totals[h - 1]) if h else near_half[h]
            normed_two.append(with_sibling(normed_near))
            pair = mm(normed_two[h], gate_up, ((1,), (0,)))
            gate, upward = pair[:, :units], pair[:, units:]
            sigmoid_gate = jax.nn.sigmoid(gate)
            activated = gate * sigmoid_gate
            hidden.append((activated * upward).astype(BF16))
            grad_hidden = mm(grad_out[h], down, ((1,), (1,)))
            slope = sigmoid_gate * (1.0 + gate * (1.0 - sigmoid_gate))
            grad_gate = (grad_hidden * upward * slope).astype(BF16)
            grad_up = (grad_hidden * activated).astype(BF16)
            both_grads = jnp.concatenate([grad_gate, grad_up], axis=1)
            grad_pair.append(both_grads)
            if not h:
                both_grads = after(both_grads, near_half[-1])

            def two_product(near, both_grads=both_grads):
                return mm(both_grads[near * half : (near + 1) * half], gate_up, ((1,), (1,)))

            two_totals.append(near_total(two_product)[0])
            total = two_totals[h] if not h else after(two_totals[h], two_parts[h - 1])
            two_parts.append(
                lax.psum_scatter(total, "narrow", scatter_dimension=0, tiled=True)
            )

        for h in range(HALVES):
            late_hidden = after(hidden[h], two_totals[-1], two_parts[0])

            def branch_product(near, late_hidden=late_hidden):
                return mm(late_hidden[near * half : (near + 1) * half], down, ((1,), (0,)))

            branch_totals.append(near_total(branch_product)[0])

        pair_term = mm(
            jnp.concatenate(normed_two, axis=0), jnp.concatenate(grad_pair, axis=0), ((0,), (0,))
        ).astype(BF16)
        pair_sum = lax.psum_scatter(
            after(pair_term, two_parts[-1], branch_totals[-1]), "wide", scatter_dimension=0, tiled=True,
            axis_index_groups=chip_groups,
        )

        grad_two = jnp.concatenate(two_parts, axis=0).astype(F32)
        scaled_two = jnp.concatenate(scaled_half, axis=0)
        factor_two = jnp.concatenate(factor_half, axis=0)
        grad_scaled_two = grad_two * gain_two
        grad_middle = grad_out_own.astype(F32) + factor_two * (
            grad_scaled_two
            - scaled_two * jnp.mean(grad_scaled_two * scaled_two, axis=-1, keepdims=True)
        )
        middle_parts = fan_out(grad_middle.astype(BF16), outer_swap, outer)
        branch_total = jnp.stack(
            [total.reshape(narrow, piece, model) for total in branch_totals], axis=1
        ).reshape(-1, model)
        branch_parts = narrow_sum(after(branch_total, middle_parts[0]))
        after_attention = jnp.concatenate(after_half, axis=0)
        layer_output = after_attention + jnp.sum(branch_parts.astype(F32), axis=0)
        down_term = mm(
            jnp.concatenate([after(hidden[0], middle_parts[0])] + hidden[1:], axis=0),
            jnp.stack([after(first, middle_parts[1]), first_far], axis=1).reshape(-1, model),
            ((0,), (0,)),
        ).astype(BF16)
        middle_parts[0] = after(middle_parts[0], down_term)
        near_middle = lax.optimization_barrier(jnp.concatenate(middle_parts, axis=0))
        grad_attention = after(with_sibling(near_middle), branch_parts)
        out_term = mm(mixed, grad_attention, ((1,), (0,))).astype(BF16)
        out_term = out_term.reshape(narrow, rows, model)
        out_split = [pick(out_term, layer ^ step) for step in range(narrow)]
        out_sent = [narrow_swap(out_split[step], step) for step in range(1, narrow)]
        grad_mixed = mm(out_own, after(grad_attention, *out_split), ((1,), (1,)))
        grad_mixed = grad_mixed.astype(BF16)
        grad_lin = attend_back(
            place_arg, grad_mixed.reshape(heads, HEAD, -1), query, key, value, lse, cosine, sine,
            keydoc, doc, tokens, outer,
        ).reshape(cols, -1)
        grad_lin = after(grad_lin, *out_sent)

        lin_term = mm(normed_one, grad_lin, ((0,), (1,))).astype(BF16)
        lin_term = lin_term.reshape(wide, narrow, rows, cols).transpose(1, 0, 2, 3)
        late_lin = after(grad_lin, lin_term)

        def one_product(near):
            return mm(late_lin[:, near * own : (near + 1) * own], attention_weight, ((0,), (1,)))

        one_total, _ = near_total(one_product)
        one_parts = scatter(one_total, outer_swap, outer)
        grad_one = add_up(one_parts)
        scaled_one, factor_one = normalize(residual)
        grad_scaled_one = grad_one * gain_one
        input_grad = grad_middle + factor_one * (
            grad_scaled_one
            - scaled_one * jnp.mean(grad_scaled_one * scaled_one, axis=-1, keepdims=True)
        )

        out_grad = add_up([after(out_split[0], lin_term)] + out_sent)
        lin_near = after(lax.all_to_all(lin_term, "narrow", 0, 0, tiled=True), one_parts[0])
        lin_sum = jnp.sum(lin_near.astype(F32), axis=0)
        lin_split = lin_sum.astype(BF16).reshape(outer, INNER, rows, cols)
        mine = pick(lin_split, core, 1)
        other = core_swap(pick(lin_split, 1 - core, 1))
        lin_pair = jnp.stack([mine, other], axis=1)
        lin_parts = [pick(lin_pair, chip)] + [
            outer_swap(pick(lin_pair, chip ^ step), step) for step in range(1, outer)
        ]
        lin_parts = jnp.concatenate(lin_parts, axis=0)
        lin_grad = jnp.stack([pick(lin_parts, place ^ w) for w in range(wide)]).astype(F32)
        down_grad = lax.psum_scatter(
            after(down_term, pair_sum, lin_sum, one_total), "wide", scatter_dimension=0, tiled=True,
            axis_index_groups=chip_groups,
        ).astype(F32)

        pair_sum = after(pair_sum, lin_sum).reshape(near_size, rows, pair_cols)
        pair_grad = lax.all_to_all(pair_sum, both, 0, 0, axis_index_groups=near_groups, tiled=True)
        if down_rows % 128 == 0:
            gate_grad, up_grad, gain_sum = join_pair(
                pair_grad, after(gate_weight, down_grad), up_weight, outer, down_rows
            )
            gain_sum = gain_sum[:, 0]
        else:
            pair_grad = pair_grad.reshape(near_size, rows, 2, outer, down_rows)
            pair_grad = pair_grad.transpose(2, 1, 3, 0, 4).reshape(2, rows, -1).astype(F32)
            gate_grad, up_grad = pair_grad[0], pair_grad[1]
            gain_sum = jnp.sum(gate_grad * gate_weight.astype(F32), axis=1) + jnp.sum(
                up_grad * up_weight.astype(F32), axis=1
            )
        gain_two_grad = gain_sum / feedforward_gain.astype(F32)

        query_grad = lin_grad[:, :, :head_cols].transpose(1, 0, 2).reshape(rows, -1)

        def kv_join(part):
            joined = part.reshape(wide // repeat, repeat, rows, kv_cols).sum(axis=1)
            return joined.transpose(1, 0, 2).reshape(rows, -1)

        key_grad = kv_join(lin_grad[:, :, head_cols : head_cols + kv_cols])
        value_grad = kv_join(lin_grad[:, :, head_cols + kv_cols :])
        gain_one_grad = (
            jnp.sum(query_grad * query_weight.astype(F32), axis=1)
            + jnp.sum(key_grad * key_weight.astype(F32), axis=1)
            + jnp.sum(value_grad * value_weight.astype(F32), axis=1)
        ) / attention_gain.astype(F32)
        return (
            layer_output[None].astype(BF16),
            input_grad[None].astype(BF16),
            gain_one_grad,
            query_grad,
            key_grad,
            value_grad,
            out_grad,
            gain_two_grad,
            gate_grad,
            up_grad,
            down_grad,
        )

    return per_device


def solution(mesh):
    rows = P(("wide", "narrow"), None)
    line = P(("wide", "narrow"))
    stream = P("narrow", "wide", None)
    return jax.shard_map(
        make_program(mesh.shape["wide"], mesh.shape["narrow"]),
        mesh=mesh,
        in_specs=(
            stream, stream, P("narrow", None), P("narrow", None),
            line, rows, rows, rows, rows, line, rows, rows, rows,
        ),
        out_specs=(stream, stream, line, rows, rows, rows, rows, line, rows, rows, rows),
        check_vma=False,
    )
```

```python
import functools

import jax
import jax.numpy as jnp
import numpy as np
from jax import lax
from jax.experimental import pallas as pl
from jax.experimental.pallas import tpu as pltpu
from jax.sharding import PartitionSpec as P

HEADS = 32
HEAD = 64
DOCS = 3
EPSILON = 1e-05
MASKED = -1e30
INNER = 2
HALVES = 2
F32 = jnp.float32
BF16 = jnp.bfloat16


def inverse_rates(head_width):
    plain = 500000.0 ** (-(np.arange(0, head_width, 2) * 1.0) / head_width)
    wavelength = 2.0 * np.pi / plain
    smooth = (8192.0 / wavelength - 1.0) / 3.0
    blended = (1.0 - smooth) * plain / 32.0 + smooth * plain
    scaled = np.where(
        wavelength > 8192.0, plain / 32.0, np.where(wavelength < 2048.0, plain, blended)
    )
    return scaled.astype(np.float32)


def stream_positions(documents):
    numbers = jnp.arange(DOCS, dtype=jnp.int32)
    starts = jnp.sum((documents[None, :] < numbers[:, None]).astype(jnp.int32), axis=1)
    own_start = jnp.sum(
        jnp.where(documents[:, None] == numbers[None, :], starts[None, :], 0), axis=1
    )
    return jnp.arange(documents.shape[0], dtype=jnp.int32) - own_start


def normalize(values):
    factor = lax.rsqrt(jnp.mean(values * values, axis=-1, keepdims=True) + EPSILON)
    return values * factor, factor


def mm(left, right, dims):
    return lax.dot_general(left, right, (dims, ((), ())), preferred_element_type=F32)


def block_offset(place, block, outer, tokens):
    peer = place ^ block
    return pl.multiple_of(((peer % INNER) * outer + peer // INNER) * tokens, tokens)


def fill_bias(bias_ref, keydoc_ref, doc_ref, start, width, length):
    shape = (length, width)
    key_index = lax.broadcasted_iota(jnp.int32, shape, 0)
    query_index = lax.broadcasted_iota(jnp.int32, shape, 1) + start
    allowed = (keydoc_ref[0:length, :] == doc_ref[:, start : start + width]) & (
        key_index <= query_index
    )
    bias_ref[0:length, :] = jnp.where(allowed, 0.0, MASKED)


def attend_kernel(
    heads, tokens, outer, width,
    place_ref, lin_ref, cos_ref, sin_ref, keydoc_ref, doc_ref,
    mixed_ref, query_ref, key_ref, value_ref, lse_ref,
    key_rows, bias_ref,
):
    length = doc_ref.shape[1]
    key_heads = key_ref.shape[0]
    group = heads // key_heads
    half = HEAD // 2
    place = place_ref[0]
    for block in range(length // tokens):
        source = pl.ds(block_offset(place, block, outer, tokens), tokens)
        lanes = slice(block * tokens, (block + 1) * tokens)
        cosine, sine = cos_ref[:, lanes], sin_ref[:, lanes]
        for head in range(heads + key_heads):
            first = lin_ref[head, 0:half, source]
            second = lin_ref[head, half:HEAD, source]
            one = (first * cosine - second * sine).astype(BF16)
            two = (second * cosine + first * sine).astype(BF16)
            if head < heads:
                scale = jnp.asarray(HEAD ** (-0.5), BF16)
                query_ref[head, 0:half, lanes] = one * scale
                query_ref[head, half:HEAD, lanes] = two * scale
            else:
                key_ref[head - heads, 0:half, lanes] = one
                key_ref[head - heads, half:HEAD, lanes] = two
        for head in range(key_heads):
            value_ref[head, :, lanes] = lin_ref[heads + key_heads + head, :, source].astype(BF16)
    for kv in range(key_heads):
        key_rows[kv] = key_ref[kv].astype(F32).T.astype(BF16)
    for step in range(length // width):
        start = step * width
        reach = start + width
        fill_bias(bias_ref, keydoc_ref, doc_ref, start, width, reach)
        for kv in range(key_heads):

            def one_head(index, carry, kv=kv, start=start, reach=reach):
                head = kv * group + index
                query = query_ref[head, :, start:reach]
                scores = mm(key_rows[kv, 0:reach, :], query, ((1,), (0,))) + bias_ref[0:reach, :]
                top = jnp.max(scores, axis=0, keepdims=True)
                terms = jnp.exp(scores - top)
                total = jnp.sum(terms, axis=0, keepdims=True)
                probs = (terms * (1.0 / total)).astype(BF16)
                mixed = mm(value_ref[kv, :, 0:reach], probs, ((1,), (0,))).astype(BF16)
                for block in range(start // tokens, reach // tokens):
                    target = pl.ds(block_offset(place, block, outer, tokens), tokens)
                    lanes = slice(block * tokens - start, (block + 1) * tokens - start)
                    mixed_ref[head, :, target] = mixed[:, lanes]
                lse_ref[head, :, start:reach] = top + jnp.log(total)
                return carry

            lax.fori_loop(0, group, one_head, 0)


def attend_back_kernel(
    heads, tokens, outer, width,
    place_ref, grad_ref, query_ref, key_ref, value_ref, lse_ref, cos_ref, sin_ref,
    keydoc_ref, doc_ref,
    out_ref,
    key_rows, value_rows, key_grad, value_grad, grad_abs, bias_ref,
):
    length = doc_ref.shape[1]
    key_heads = key_ref.shape[0]
    group = heads // key_heads
    half = HEAD // 2
    scale = HEAD ** (-0.5)
    place = place_ref[0]

    def put_back(head, block, gradient):
        target = pl.ds(block_offset(place, block, outer, tokens), tokens)
        lanes = slice(block * tokens, (block + 1) * tokens)
        cosine, sine = cos_ref[:, lanes], sin_ref[:, lanes]
        one, two = gradient[0:half], gradient[half:HEAD]
        out_ref[head, 0:half, target] = (one * cosine + two * sine).astype(BF16)
        out_ref[head, half:HEAD, target] = (two * cosine - one * sine).astype(BF16)

    for block in range(length // tokens):
        source = pl.ds(block_offset(place, block, outer, tokens), tokens)
        lanes = slice(block * tokens, (block + 1) * tokens)
        for head in range(heads):
            grad_abs[head, :, lanes] = grad_ref[head, :, source]
    for kv in range(key_heads):
        key_rows[kv] = key_ref[kv].astype(F32).T.astype(BF16)
        value_rows[kv] = value_ref[kv].astype(F32).T.astype(BF16)
    key_grad[...] = jnp.zeros_like(key_grad)
    value_grad[...] = jnp.zeros_like(value_grad)
    for step in range(length // width):
        start = step * width
        reach = start + width
        fill_bias(bias_ref, keydoc_ref, doc_ref, start, width, reach)
        for kv in range(key_heads):

            def one_head(index, carry, kv=kv, start=start, reach=reach):
                head = kv * group + index
                query = query_ref[head, :, start:reach]
                grad = grad_abs[head, :, start:reach]
                query_rows = query.astype(F32).T.astype(BF16)
                grad_rows = grad.astype(F32).T.astype(BF16)
                scores = mm(key_rows[kv, 0:reach, :], query, ((1,), (0,))) + bias_ref[0:reach, :]
                probs = jnp.exp(scores - lse_ref[head, :, start:reach])
                grad_probs = mm(value_rows[kv, 0:reach, :], grad, ((1,), (0,)))
                delta = jnp.sum(probs * grad_probs, axis=0, keepdims=True)
                grad_scores = (probs * (grad_probs - delta)).astype(BF16)
                value_grad[kv, 0:reach, :] += mm(probs.astype(BF16), grad_rows, ((1,), (0,)))
                key_grad[kv, 0:reach, :] += mm(grad_scores, query_rows, ((1,), (0,)))
                grad_query = mm(key_ref[kv, :, 0:reach], grad_scores, ((1,), (0,))) * scale
                for block in range(start // tokens, reach // tokens):
                    lanes = slice(block * tokens - start, (block + 1) * tokens - start)
                    put_back(head, block, grad_query[:, lanes])
                return carry

            lax.fori_loop(0, group, one_head, 0)
    for block in range(length // tokens):
        lanes = slice(block * tokens, (block + 1) * tokens)
        target = pl.ds(block_offset(place, block, outer, tokens), tokens)
        for kv in range(key_heads):
            put_back(heads + kv, block, key_grad[kv, lanes, :].T)
            out_ref[heads + key_heads + kv, :, target] = value_grad[kv, lanes, :].T.astype(BF16)


def vmem_spec():
    return pl.BlockSpec(memory_space=pltpu.VMEM)


def attend(place, lin, cosine, sine, keydoc, doc, heads, tokens, outer):
    total, _, length = lin.shape
    key_heads = (total - heads) // 2
    width = min(256, length)
    shape = jax.ShapeDtypeStruct
    return pl.pallas_call(
        functools.partial(attend_kernel, heads, tokens, outer, width),
        out_shape=(
            shape((heads, HEAD, length), BF16),
            shape((heads, HEAD, length), BF16),
            shape((key_heads, HEAD, length), BF16),
            shape((key_heads, HEAD, length), BF16),
            shape((heads, 1, length), F32),
        ),
        in_specs=[pl.BlockSpec(memory_space=pltpu.SMEM)] + [vmem_spec()] * 5,
        out_specs=(vmem_spec(),) * 5,
        scratch_shapes=[
            pltpu.VMEM((key_heads, length, HEAD), BF16),
            pltpu.VMEM((length, width), F32),
        ],
        compiler_params=pltpu.CompilerParams(vmem_limit_bytes=40 * 2**20),
        cost_estimate=pl.CostEstimate(
            flops=heads * length * HEAD,
            bytes_accessed=total * HEAD * length,
            transcendentals=0,
        ),
    )(place, lin, cosine, sine, keydoc, doc)


def attend_back(place, grad, query, key, value, lse, cosine, sine, keydoc, doc, tokens, outer):
    heads, _, length = query.shape
    key_heads = key.shape[0]
    width = min(256, length)
    total = heads + 2 * key_heads
    return pl.pallas_call(
        functools.partial(attend_back_kernel, heads, tokens, outer, width),
        out_shape=jax.ShapeDtypeStruct((total, HEAD, length), BF16),
        in_specs=[pl.BlockSpec(memory_space=pltpu.SMEM)] + [vmem_spec()] * 9,
        out_specs=vmem_spec(),
        scratch_shapes=[
            pltpu.VMEM((key_heads, length, HEAD), BF16),
            pltpu.VMEM((key_heads, length, HEAD), BF16),
            pltpu.VMEM((key_heads, length, HEAD), F32),
            pltpu.VMEM((key_heads, length, HEAD), F32),
            pltpu.VMEM((heads, HEAD, length), BF16),
            pltpu.VMEM((length, width), F32),
        ],
        compiler_params=pltpu.CompilerParams(vmem_limit_bytes=40 * 2**20),
        cost_estimate=pl.CostEstimate(
            flops=heads * length * HEAD,
            bytes_accessed=total * HEAD * length,
            transcendentals=0,
        ),
    )(place, grad, query, key, value, lse, cosine, sine, keydoc, doc)


def join_kernel(down_rows, gate_part, up_part, gate_weight, up_weight, gate_ref, up_ref, sum_ref):
    @pl.when(pl.program_id(0) == 0)
    def _():
        sum_ref[...] = jnp.zeros_like(sum_ref)

    for part, weight, out in ((gate_part, gate_weight, gate_ref), (up_part, up_weight, up_ref)):
        for block in range(part.shape[0]):
            lanes = slice(block * down_rows, (block + 1) * down_rows)
            piece = part[block].astype(F32)
            out[:, lanes] = piece
            term = piece * weight[:, lanes].astype(F32)
            sum_ref[...] += jnp.sum(term, axis=1, keepdims=True)


def join_pair(pair_grad, gate_weight, up_weight, outer, down_rows):
    blocks, rows, _ = pair_grad.shape
    units = gate_weight.shape[1]
    width = blocks * down_rows
    shape = jax.ShapeDtypeStruct
    wide_spec = pl.BlockSpec((rows, width), lambda i: (0, i))
    return pl.pallas_call(
        functools.partial(join_kernel, down_rows),
        grid=(outer,),
        out_shape=(
            shape((rows, units), F32), shape((rows, units), F32), shape((rows, 128), F32),
        ),
        in_specs=[
            pl.BlockSpec((blocks, rows, down_rows), lambda i: (0, 0, i)),
            pl.BlockSpec((blocks, rows, down_rows), lambda i: (0, 0, i + outer)),
            wide_spec,
            wide_spec,
        ],
        out_specs=(wide_spec, wide_spec, pl.BlockSpec((rows, 128), lambda i: (0, 0))),
        compiler_params=pltpu.CompilerParams(vmem_limit_bytes=32 * 2**20),
        cost_estimate=pl.CostEstimate(
            flops=4 * rows * units, bytes_accessed=16 * rows * units, transcendentals=0
        ),
    )(pair_grad, pair_grad, gate_weight, up_weight)


def exchange(value, axis, size, step):
    return lax.ppermute(value, axis, [(i, i ^ step) for i in range(size)])


def put(buffer, piece, index):
    return lax.dynamic_update_slice(
        buffer, piece, tuple(jnp.asarray(i, jnp.int32) for i in index)
    )


def pick(value, index, axis=0):
    return lax.dynamic_index_in_dim(value, index, axis, keepdims=False)


def after(value, *marks):
    return lax.optimization_barrier((value,) + marks)[0]


def make_program(wide, narrow):
    outer = wide // INNER
    near_size = INNER * narrow
    near_groups = [[o * near_size + i for i in range(near_size)] for o in range(outer)]
    chip_groups = [[c + INNER * o for o in range(outer)] for c in range(INNER)]
    both = ("wide", "narrow")

    def core_swap(value):
        return exchange(value, "wide", wide, 1)

    def outer_swap(value, step):
        return exchange(value, "wide", wide, INNER * step)

    def narrow_swap(value, step):
        return exchange(value, "narrow", narrow, step)

    def fan_out(value, swap, size):
        return [value] + [swap(value, step) for step in range(1, size)]

    def narrow_gather(value):
        spread = jnp.broadcast_to(value[None], (narrow,) + value.shape)
        return lax.all_to_all(spread, "narrow", 0, 0, tiled=True)

    def narrow_sum(total):
        split = total.reshape(narrow, -1, total.shape[-1])
        return lax.all_to_all(split, "narrow", 0, 0, tiled=True)

    def with_sibling(first):
        return jnp.concatenate([first, core_swap(first)], axis=0)

    def join_near(parts):
        first = jnp.concatenate(parts, axis=0)
        return jnp.concatenate([first, core_swap(first)], axis=0)

    def near_total(product):
        arrived = core_swap(product(1).astype(BF16))
        return (product(0) + arrived.astype(F32)).astype(BF16), arrived

    def scatter(total, swap, size):
        split = total.reshape(size, -1, total.shape[-1])
        return [split[0]] + [swap(split[step], step) for step in range(1, size)]

    def add_up(parts):
        total = parts[0].astype(F32)
        for piece in parts[1:]:
            total = total + piece.astype(F32)
        return total

    def per_device(
        layer_input, output_grad, doc_ids, keep_mask, attention_gain, query_weight, key_weight,
        value_weight, out_weight, feedforward_gain, gate_weight, up_weight, down_weight,
    ):
        tokens = layer_input.shape[1]
        model = layer_input.shape[2]
        rows = query_weight.shape[0]
        down_rows = down_weight.shape[0]
        kv_total = key_weight.shape[1] // HEAD
        heads = HEADS // wide
        group = HEADS // kv_total
        key_heads = max(1, heads // group)
        repeat = max(1, group // heads)
        place = lax.axis_index("wide")
        chip = place // INNER
        layer = lax.axis_index("narrow")
        core = place % INNER
        place_arg = place.reshape(1).astype(jnp.int32)

        head_cols = heads * HEAD
        kv_cols = key_heads * HEAD

        def kv_split(weight):
            parts = weight.reshape(rows, -1, kv_cols)
            return jnp.repeat(parts, repeat, axis=1)

        packed = jnp.concatenate(
            [query_weight.reshape(rows, wide, head_cols), kv_split(key_weight), kv_split(value_weight)],
            axis=2,
        )
        cols = packed.shape[2]
        own_input = layer_input[0]
        residual = own_input.astype(F32)
        out_parts = fan_out(out_weight, narrow_swap, narrow)
        packed = packed.transpose(1, 0, 2)
        gain_rows = -(-2 * rows // cols) * 8
        gains = jnp.concatenate([attention_gain, feedforward_gain])
        gains = jnp.pad(gains, (0, gain_rows * cols - 2 * rows)).reshape(1, gain_rows, cols)
        gains = jnp.broadcast_to(gains, (wide, gain_rows, cols))
        packed = jnp.concatenate([packed, gains], axis=1)
        by_wide = lax.all_to_all(packed, "wide", 0, 0, tiled=True)
        input_parts = fan_out(after(own_input, by_wide), outer_swap, outer)

        weight_parts = fan_out(after(by_wide, *out_parts), narrow_swap, narrow)

        def for_group(weight):
            return weight.reshape(rows, outer, near_size, down_rows).transpose(2, 0, 1, 3)

        pair_cols = 2 * outer * down_rows
        units = pair_cols // 2
        pair_weight = jnp.stack([for_group(gate_weight), for_group(up_weight)], axis=2)
        pair_weight = pair_weight.reshape(near_size, rows, pair_cols)
        pair_weight = after(pair_weight, *weight_parts, *input_parts)
        column = lax.all_to_all(
            pair_weight, both, 0, 0, axis_index_groups=near_groups, tiled=True
        )
        down = lax.all_gather(
            down_weight, "wide", axis=0, tiled=True, axis_index_groups=chip_groups
        )

        all_input = join_near(input_parts)
        scaled_all, factor_all = normalize(all_input.astype(F32))
        attention_weight = after(jnp.zeros((wide, narrow, rows, cols), BF16), factor_all)
        for step, piece in enumerate(weight_parts):
            attention_weight = put(
                attention_weight, piece[:, None, :rows], (0, layer ^ step, 0, 0)
            )
        attention_weight = attention_weight.reshape(model, cols)
        lines = jnp.stack([piece[:, rows, : 2 * rows] for piece in weight_parts], axis=1)
        lines = jnp.stack([pick(lines, layer ^ step, 1) for step in range(narrow)], axis=1)
        lines = lines.astype(F32)
        gain_one = lines[:, :, :rows].reshape(1, model)
        gain_two = lines[:, :, rows:].reshape(1, model)

        out_own = jnp.zeros((narrow, rows, model), BF16)
        for step, piece in enumerate(out_parts):
            out_own = put(out_own, piece[None], (layer ^ step, 0, 0))
        out_own = out_own.reshape(narrow * rows, model)

        grad_out_own = output_grad[0]
        grad_out_near = narrow_gather(after(grad_out_own, column)).reshape(-1, model)

        own = all_input.shape[0] // INNER
        documents = doc_ids[0]
        positions = stream_positions(documents)
        angles = jnp.asarray(inverse_rates(HEAD))[:, None] * positions.astype(F32)[None, :]
        cosine, sine = jnp.cos(angles), jnp.sin(angles)
        keydoc = jnp.where(keep_mask[0] > 0, documents, -1)[:, None]
        doc = documents[None, :]
        normed_one = (scaled_all * gain_one).astype(BF16)
        lin = mm(attention_weight, normed_one, ((0,), (1,)))
        lin = lin.reshape(-1, HEAD, lin.shape[1])
        mixed, query, key, value, lse = attend(
            place_arg, lin, cosine, sine, keydoc, doc, heads, tokens, outer
        )
        mixed = mixed.reshape(head_cols, -1)

        def out_product(near):
            return mm(mixed[:, near * own : (near + 1) * own], out_own, ((0,), (0,)))

        attended, _ = near_total(out_product)
        gate_up = lax.all_gather(
            after(column.reshape(near_size * rows, pair_cols), down, attended), "wide",
            axis=0, tiled=True, axis_index_groups=chip_groups,
        )
        piece = tokens // HALVES
        attended = attended.reshape(outer, HALVES, piece, model)
        residual_half = residual.reshape(HALVES, piece, model)
        after_half, scaled_half, factor_half, normed_half = [], [], [], []
        attended_parts = [
            [attended[0, h]] + [outer_swap(attended[step, h], step) for step in range(1, outer)]
            for h in range(HALVES)
        ]
        attended_parts[0][0] = after(attended_parts[0][0], grad_out_near)
        for h in range(HALVES):
            after_half.append(residual_half[h] + add_up(attended_parts[h]))
            scaled, factor = normalize(after_half[h])
            scaled_half.append(scaled)
            factor_half.append(factor)
            normed_half.append((scaled * gain_two).astype(BF16))

        half = narrow * piece
        first = grad_out_near.reshape(narrow, HALVES, piece, model).transpose(1, 0, 2, 3)
        first_far = core_swap(first)
        grad_out = jnp.stack([first, first_far], axis=1).reshape(HALVES, -1, model)
        normed_two, hidden, grad_pair, two_totals, two_parts, branch_totals = [], [], [], [], [], []
        near_half = [narrow_gather(normed_half[h]).reshape(-1, model) for h in range(HALVES)]
        for h in range(HALVES):
            normed_near = after(near_half[h], two_totals[h - 1]) if h else near_half[h]
            normed_two.append(with_sibling(normed_near))
            pair = mm(normed_two[h], gate_up, ((1,), (0,)))
            gate, upward = pair[:, :units], pair[:, units:]
            sigmoid_gate = jax.nn.sigmoid(gate)
            activated = gate * sigmoid_gate
            hidden.append((activated * upward).astype(BF16))
            grad_hidden = mm(grad_out[h], down, ((1,), (1,)))
            slope = sigmoid_gate * (1.0 + gate * (1.0 - sigmoid_gate))
            grad_gate = (grad_hidden * upward * slope).astype(BF16)
            grad_up = (grad_hidden * activated).astype(BF16)
            both_grads = jnp.concatenate([grad_gate, grad_up], axis=1)
            grad_pair.append(both_grads)
            if not h:
                both_grads = after(both_grads, near_half[-1])

            def two_product(near, both_grads=both_grads):
                return mm(both_grads[near * half : (near + 1) * half], gate_up, ((1,), (1,)))

            two_totals.append(near_total(two_product)[0])
            total = two_totals[h] if not h else after(two_totals[h], two_parts[h - 1])
            two_parts.append(
                lax.psum_scatter(total, "narrow", scatter_dimension=0, tiled=True)
            )

        for h in range(HALVES):
            late_hidden = after(hidden[h], two_totals[-1], two_parts[0])

            def branch_product(near, late_hidden=late_hidden):
                return mm(late_hidden[near * half : (near + 1) * half], down, ((1,), (0,)))

            branch_totals.append(near_total(branch_product)[0])

        pair_term = mm(
            jnp.concatenate(normed_two, axis=0), jnp.concatenate(grad_pair, axis=0), ((0,), (0,))
        ).astype(BF16)
        pair_sum = lax.psum_scatter(
            after(pair_term, two_parts[-1], branch_totals[-1]), "wide", scatter_dimension=0, tiled=True,
            axis_index_groups=chip_groups,
        )

        grad_two = jnp.concatenate(two_parts, axis=0).astype(F32)
        scaled_two = jnp.concatenate(scaled_half, axis=0)
        factor_two = jnp.concatenate(factor_half, axis=0)
        grad_scaled_two = grad_two * gain_two
        grad_middle = grad_out_own.astype(F32) + factor_two * (
            grad_scaled_two
            - scaled_two * jnp.mean(grad_scaled_two * scaled_two, axis=-1, keepdims=True)
        )
        middle_parts = fan_out(grad_middle.astype(BF16), outer_swap, outer)
        branch_total = jnp.stack(
            [total.reshape(narrow, piece, model) for total in branch_totals], axis=1
        ).reshape(-1, model)
        branch_parts = narrow_sum(after(branch_total, middle_parts[0]))
        after_attention = jnp.concatenate(after_half, axis=0)
        layer_output = after_attention + jnp.sum(branch_parts.astype(F32), axis=0)
        down_term = mm(
            jnp.concatenate([after(hidden[0], middle_parts[0])] + hidden[1:], axis=0),
            jnp.stack([after(first, middle_parts[1]), first_far], axis=1).reshape(-1, model),
            ((0,), (0,)),
        ).astype(BF16)
        middle_parts[0] = after(middle_parts[0], down_term)
        near_middle = lax.optimization_barrier(jnp.concatenate(middle_parts, axis=0))
        grad_attention = after(with_sibling(near_middle), branch_parts)
        out_term = mm(mixed, grad_attention, ((1,), (0,))).astype(BF16)
        out_term = out_term.reshape(narrow, rows, model)
        out_split = [pick(out_term, layer ^ step) for step in range(narrow)]
        out_sent = [narrow_swap(out_split[step], step) for step in range(1, narrow)]
        grad_mixed = mm(out_own, after(grad_attention, *out_split), ((1,), (1,)))
        grad_mixed = grad_mixed.astype(BF16)
        grad_lin = attend_back(
            place_arg, grad_mixed.reshape(heads, HEAD, -1), query, key, value, lse, cosine, sine,
            keydoc, doc, tokens, outer,
        ).reshape(cols, -1)
        grad_lin = after(grad_lin, *out_sent)

        lin_term = mm(normed_one, grad_lin, ((0,), (1,))).astype(BF16)
        lin_term = lin_term.reshape(wide, narrow, rows, cols).transpose(1, 0, 2, 3)
        late_lin = after(grad_lin, lin_term)

        def one_product(near):
            return mm(late_lin[:, near * own : (near + 1) * own], attention_weight, ((0,), (1,)))

        one_total, _ = near_total(one_product)
        one_parts = scatter(one_total, outer_swap, outer)
        grad_one = add_up(one_parts)
        scaled_one, factor_one = normalize(residual)
        grad_scaled_one = grad_one * gain_one
        input_grad = grad_middle + factor_one * (
            grad_scaled_one
            - scaled_one * jnp.mean(grad_scaled_one * scaled_one, axis=-1, keepdims=True)
        )

        out_grad = add_up([after(out_split[0], lin_term)] + out_sent)
        lin_near = after(lax.all_to_all(lin_term, "narrow", 0, 0, tiled=True), one_parts[0])
        lin_sum = jnp.sum(lin_near.astype(F32), axis=0)
        lin_split = lin_sum.astype(BF16).reshape(outer, INNER, rows, cols)
        mine = pick(lin_split, core, 1)
        other = core_swap(pick(lin_split, 1 - core, 1))
        lin_pair = jnp.stack([mine, other], axis=1)
        lin_parts = [pick(lin_pair, chip)] + [
            outer_swap(pick(lin_pair, chip ^ step), step) for step in range(1, outer)
        ]
        lin_parts = jnp.concatenate(lin_parts, axis=0)
        lin_grad = jnp.stack([pick(lin_parts, place ^ w) for w in range(wide)]).astype(F32)
        down_grad = lax.psum_scatter(
            after(down_term, pair_sum, one_parts[0]), "wide", scatter_dimension=0, tiled=True,
            axis_index_groups=chip_groups,
        ).astype(F32)

        pair_sum = after(pair_sum, lin_sum).reshape(near_size, rows, pair_cols)
        pair_grad = lax.all_to_all(pair_sum, both, 0, 0, axis_index_groups=near_groups, tiled=True)
        if down_rows % 128 == 0:
            gate_grad, up_grad, gain_sum = join_pair(
                pair_grad, after(gate_weight, down_grad), up_weight, outer, down_rows
            )
            gain_sum = gain_sum[:, 0]
        else:
            pair_grad = pair_grad.reshape(near_size, rows, 2, outer, down_rows)
            pair_grad = pair_grad.transpose(2, 1, 3, 0, 4).reshape(2, rows, -1).astype(F32)
            gate_grad, up_grad = pair_grad[0], pair_grad[1]
            gain_sum = jnp.sum(gate_grad * gate_weight.astype(F32), axis=1) + jnp.sum(
                up_grad * up_weight.astype(F32), axis=1
            )
        gain_two_grad = gain_sum / feedforward_gain.astype(F32)

        query_grad = lin_grad[:, :, :head_cols].transpose(1, 0, 2).reshape(rows, -1)

        def kv_join(part):
            joined = part.reshape(wide // repeat, repeat, rows, kv_cols).sum(axis=1)
            return joined.transpose(1, 0, 2).reshape(rows, -1)

        key_grad = kv_join(lin_grad[:, :, head_cols : head_cols + kv_cols])
        value_grad = kv_join(lin_grad[:, :, head_cols + kv_cols :])
        gain_one_grad = (
            jnp.sum(query_grad * query_weight.astype(F32), axis=1)
            + jnp.sum(key_grad * key_weight.astype(F32), axis=1)
            + jnp.sum(value_grad * value_weight.astype(F32), axis=1)
        ) / attention_gain.astype(F32)
        return (
            layer_output[None].astype(BF16),
            input_grad[None].astype(BF16),
            gain_one_grad,
            query_grad,
            key_grad,
            value_grad,
            out_grad,
            gain_two_grad,
            gate_grad,
            up_grad,
            down_grad,
        )

    return per_device


def solution(mesh):
    rows = P(("wide", "narrow"), None)
    line = P(("wide", "narrow"))
    stream = P("narrow", "wide", None)
    return jax.shard_map(
        make_program(mesh.shape["wide"], mesh.shape["narrow"]),
        mesh=mesh,
        in_specs=(
            stream, stream, P("narrow", None), P("narrow", None),
            line, rows, rows, rows, rows, line, rows, rows, rows,
        ),
        out_specs=(stream, stream, line, rows, rows, rows, rows, line, rows, rows, rows),
        check_vma=False,
    )
```
